32 devices in a mesh: dp: 4 (over x, core), expert: 8 (over z, y).
Axes of the slice: x: 2, y: 2, z: 4, core: 2. Of those that a mesh axis runs over, the one named last changes fastest.
Arguments:
- out_grad: bfloat16 [2048, 7168], P('expert', 'dp'), may hold values from -6 to 6
- inputs: bfloat16 [2048, 7168], P('expert', 'dp'), may hold values from -2.5 to 2.5
- expert_ids: int32 [2048, 8], P('expert'), may hold values from 0 to 255, as said below
- gate_weights: float32 [2048, 8], P('expert'), may hold values from 0.1 to 1
- w_gate: bfloat16 [7168, 4096], P('dp', 'expert'), may hold values from -0.0625 to 0.0625
- w_up: bfloat16 [7168, 4096], P('dp', 'expert'), may hold values from -0.0625 to 0.0625
- w_down: bfloat16 [4096, 7168], P('expert', 'dp'), may hold values from -0.125 to 0.125
Outputs:
- in_grad: bfloat16 [2048, 7168], P('expert', 'dp')
- grad_gate: bfloat16 [7168, 4096], P('dp', 'expert')
- grad_up: bfloat16 [7168, 4096], P('dp', 'expert')
The draws below stay inside these ranges and needn't reach their ends.
Inputs may be any that keep to these rules, and one draw needn't show every extreme that they name: `expert_ids`: each token names 8 different experts. Within one block of 256 consecutive tokens no expert is named by more than 12 tokens, and in every draw some expert below 2 is named by exactly 12 tokens of every block.
All inputs are finite; a program needn't handle non-finite values.
Results may differ from the reference program's by a relative error of at most 0.035.
Values may be sent and summed in bfloat16 or wider, within the bound.
No kernel may reach another device: no remote copies, remote signals or barrier semaphores. Data moves between devices by JAX's collectives and lax.ppermute only.
A program may use at most 64 MiB of HBM per device.

```python
import math
import jax
import jax.numpy as jnp
from jax import lax

D = 7168
H = 2048
TOP = 8
ROUTED = 256
TOK_DEV = 256
HSPLIT = 4
CAP = 12
EXPERTS = 2
TOKENS = 2048
N_DP = 4
N_EXPERT = 8


def draw_expert_ids(key, part):
    key = jax.random.fold_in(key, 11)
    scale_unit = TOK_DEV // 128
    leader = jax.random.randint(jax.random.fold_in(key, 1), (), 0, EXPERTS).astype(jnp.int32)
    remaining = jnp.concatenate([jnp.full((7,), 6 * scale_unit, jnp.int32), jnp.full((8,), 4 * scale_unit, jnp.int32), jnp.full((16,), 3 * scale_unit, jnp.int32)])

    def one_block(block_key):
        order_key, count_key, label_key = jax.random.split(block_key, 3)
        shuffled = jax.random.permutation(order_key, ROUTED).astype(jnp.int32)
        position = jnp.argmax(shuffled == leader)
        shuffled = jnp.roll(shuffled, -position)
        counts = jnp.concatenate([jnp.full((1,), 6 * scale_unit, jnp.int32), jax.random.permutation(count_key, remaining)])
        labels = jnp.repeat(jnp.arange(32, dtype=jnp.int32), counts, total_repeat_length=TOK_DEV)
        labels = jax.random.permutation(label_key, labels)
        table_index = labels[:, None] * TOP + jnp.arange(TOP, dtype=jnp.int32)[None, :]
        return shuffled[table_index]
    block_keys = jax.random.split(jax.random.fold_in(key, 2), N_EXPERT)
    return jax.vmap(one_block)(block_keys).reshape(TOKENS, TOP).astype(jnp.int32)


def shard_levels(own_key, extent, cuts, low, top_value):
    def one(dim, blocks):
        steps = jax.random.uniform(jax.random.fold_in(jax.random.fold_in(own_key, 6), dim), (blocks,), jnp.float32, low / len(cuts), top_value / len(cuts))
        return jnp.repeat(jnp.exp(steps), extent[dim] // blocks).reshape((-1,) + (1,) * (len(extent) - dim - 1))

    loudness = one(*cuts[0])
    for cut in cuts[1:]:
        loudness = loudness * one(*cut)
    return loudness


def centred(stream_key, extent, deviation, reach, cuts=(), held_as=jnp.bfloat16):
    array = deviation * jax.random.normal(stream_key, extent, jnp.float32)
    if cuts:
        array = array * shard_levels(stream_key, extent, cuts, -0.22, 0.18)
    return jnp.clip(array, -reach, reach).astype(held_as)


def setup_inputs(seed: int = 0) -> dict:
    key_of = jax.random.split(jax.random.key(seed), 8)
    out_grad = centred(key_of[0], (TOKENS, D), 1.0, 6.0, ((0, 8), (1, 4)))
    inputs = centred(key_of[1], (TOKENS, D), 0.35, 2.5, ((0, 8), (1, 4)))
    expert_ids = draw_expert_ids(jax.random.fold_in(key_of[7], 71), 0)
    gate_weights = jnp.clip(jnp.exp(math.log(1.0) - 2.3025851 * jax.random.uniform(key_of[3], (TOKENS, TOP), jnp.float32) ** shard_levels(key_of[3], (TOKENS, TOP), ((0, 8),), -0.2, 0.2)), 0.1, 1.0)
    w_gate = centred(key_of[4], (D, EXPERTS * H), D ** -0.5, 0.0625, ((0, 4), (1, 8)))
    w_up = centred(key_of[5], (D, EXPERTS * H), D ** -0.5, 0.0625, ((0, 4), (1, 8)))
    w_down = centred(key_of[6], (EXPERTS * H, D), H ** -0.5, 0.125, ((0, 8), (1, 4)))
    return dict(out_grad=out_grad, inputs=inputs, expert_ids=expert_ids, gate_weights=gate_weights, w_gate=w_gate, w_up=w_up, w_down=w_down)


def routes(block_ids, block_gates, experts):
    tokens = block_ids.shape[0]
    flat_ids = block_ids.reshape(-1)
    matches = (flat_ids[:, None] == jnp.arange(experts, dtype=jnp.int32)[None, :]).astype(jnp.int32)
    before = jnp.cumsum(matches, axis=0) - matches
    slot_index = jnp.sum(before * matches, axis=1)
    kept_mask = jnp.sum(matches, axis=1)
    target = jnp.where(kept_mask > 0, flat_ids * CAP + slot_index, -1)
    columns = jnp.arange(experts * CAP, dtype=jnp.int32)
    onehot = (target[:, None] == columns[None, :]).astype(jnp.float32)
    weighted = onehot * block_gates.reshape(-1)[:, None]
    chosen = jnp.sum(onehot.reshape(tokens, TOP, -1), axis=1)
    scaled = jnp.sum(weighted.reshape(tokens, TOP, -1), axis=1)
    return chosen, scaled


def block_sum(left, right):
    parts = jnp.einsum('rjd,jdh->jrh', left, right)
    rounded = lax.optimization_barrier(parts.astype(jnp.bfloat16))
    return jnp.sum(rounded.astype(jnp.float32), axis=0)


def expert_backward(operands):
    grad_rows, input_rows, gate_cols, up_cols, down_rows = operands
    row_count = grad_rows.shape[0]
    feature_block = D // N_DP
    quarter_width = H // HSPLIT
    grad_split = grad_rows.astype(jnp.float32).reshape(row_count, N_DP, feature_block)
    input_split = input_rows.astype(jnp.float32).reshape(row_count, N_DP, feature_block)
    down_split = down_rows.astype(jnp.float32).reshape(H, N_DP, feature_block).transpose(1, 2, 0)
    hidden_grad = block_sum(grad_split, down_split)
    gate_pre = block_sum(input_split, gate_cols.astype(jnp.float32).reshape(N_DP, feature_block, H))
    up_pre = block_sum(input_split, up_cols.astype(jnp.float32).reshape(N_DP, feature_block, H))
    sigma = jax.nn.sigmoid(gate_pre)
    grad_gate_pre = (hidden_grad * up_pre * sigma * (1.0 + gate_pre * (1.0 - sigma))).astype(jnp.bfloat16)
    grad_up_pre = (hidden_grad * gate_pre * sigma).astype(jnp.bfloat16)
    gate_q = grad_gate_pre.astype(jnp.float32).reshape(row_count, HSPLIT, quarter_width)
    up_q = grad_up_pre.astype(jnp.float32).reshape(row_count, HSPLIT, quarter_width)
    quarters = jnp.einsum('rqh,dqh->qrd', gate_q, gate_cols.astype(jnp.float32).reshape(D, HSPLIT, quarter_width))
    quarters = quarters + jnp.einsum('rqh,dqh->qrd', up_q, up_cols.astype(jnp.float32).reshape(D, HSPLIT, quarter_width))
    rounded = lax.optimization_barrier(quarters.astype(jnp.bfloat16))
    returned = jnp.sum(rounded.astype(jnp.float32), axis=0)
    grad_gate = jnp.dot(input_rows.T, grad_gate_pre, preferred_element_type=jnp.float32).astype(jnp.bfloat16)
    grad_up = jnp.dot(input_rows.T, grad_up_pre, preferred_element_type=jnp.float32).astype(jnp.bfloat16)
    return returned, grad_gate, grad_up


def reference(out_grad, inputs, expert_ids, gate_weights, w_gate, w_up, w_down):
    blocks = N_EXPERT
    experts = EXPERTS
    row_count = blocks * CAP
    routed_ids = expert_ids.reshape(blocks, TOK_DEV, TOP)
    gate_blocks = gate_weights.reshape(blocks, TOK_DEV, TOP)
    chosen, scaled = jax.vmap(lambda a, b: routes(a, b, experts))(routed_ids, gate_blocks)
    grad_rows = out_grad.astype(jnp.float32).reshape(blocks, TOK_DEV, D)
    input_rows = inputs.astype(jnp.float32).reshape(blocks, TOK_DEV, D)
    sent_grad = jnp.einsum('btr,btd->rbd', scaled, grad_rows, precision=lax.Precision.HIGHEST).astype(jnp.bfloat16)
    sent_input = jnp.einsum('btr,btd->rbd', chosen, input_rows, precision=lax.Precision.HIGHEST).astype(jnp.bfloat16)
    sent_grad = sent_grad.reshape(experts, CAP, blocks, D).transpose(0, 2, 1, 3).reshape(experts, row_count, D)
    sent_input = sent_input.reshape(experts, CAP, blocks, D).transpose(0, 2, 1, 3).reshape(experts, row_count, D)
    gate_cols = w_gate.reshape(D, experts, H).transpose(1, 0, 2)
    up_cols = w_up.reshape(D, experts, H).transpose(1, 0, 2)
    down_rows = w_down.reshape(experts, H, D)
    returned, grad_gate, grad_up = lax.map(expert_backward, (sent_grad, sent_input, gate_cols, up_cols, down_rows))
    returned = returned.reshape(experts, blocks, CAP, D).transpose(1, 0, 2, 3).reshape(blocks, experts * CAP, D)
    in_grad = jnp.einsum('btr,brd->btd', chosen, returned, precision=lax.Precision.HIGHEST)
    in_grad = in_grad.reshape(TOKENS, D).astype(jnp.bfloat16)
    grad_gate = grad_gate.transpose(1, 0, 2).reshape(D, experts * H)
    grad_up = grad_up.transpose(1, 0, 2).reshape(D, experts * H)
    return in_grad, grad_gate, grad_up
```

```python
import functools

import jax
import jax.numpy as jnp
from jax import lax
from jax.experimental import pallas as pl
from jax.experimental.pallas import tpu as pltpu
from jax.sharding import PartitionSpec as P

HSPLIT = 4
CAP = 12
F32 = jnp.float32
BF16 = jnp.bfloat16
VMEM = pl.BlockSpec(memory_space=pltpu.VMEM)
HBM = pl.BlockSpec(memory_space=pltpu.HBM)
ANY = pl.BlockSpec(memory_space=pl.ANY)


def shape(dims, dtype=BF16):
    return jax.ShapeDtypeStruct(dims, dtype)


def run(body, outs, specs, flops, nbytes, *args, out_spec=VMEM, scratch=()):
    return pl.pallas_call(
        body,
        out_shape=outs,
        in_specs=specs,
        out_specs=out_spec if isinstance(out_spec, tuple) else jax.tree.map(lambda _: out_spec, outs),
        scratch_shapes=scratch,
        compiler_params=pltpu.CompilerParams(vmem_limit_bytes=40 * 1024 * 1024),
        cost_estimate=pl.CostEstimate(flops=flops, bytes_accessed=nbytes, transcendentals=0),
    )(*args)


def in_hbm(value):
    return pltpu.with_memory_space_constraint(value, pltpu.HBM)


def dot(left, right, left_dim=1, right_dim=0):
    return lax.dot_general(
        left, right, (((left_dim,), (right_dim,)), ((), ())), preferred_element_type=F32
    )


def iota(dims, dim):
    return lax.broadcasted_iota(jnp.int32, dims, dim)


def over_cap(rows):
    return jnp.floor((rows.astype(F32) + 0.5) * (1.0 / CAP)).astype(jnp.int32)


def core_columns(width, far):
    side = lax.rem(lax.axis_index("dp"), 2)
    side = 1 - side if far else side
    return pl.ds(pl.multiple_of(side * width, width), width)


def fold_of(width):
    return 2 if width % 256 == 0 else 1


def pick_body(experts, fold, ids_hbm, gates_hbm, grads_hbm, inputs_hbm, *refs):
    picks, pieces = refs[:fold], refs[fold : fold + experts]
    ids, gates, grads, inputs, sems = refs[fold + experts :]
    loads = [
        pltpu.make_async_copy(source, target, sems.at[place])
        for place, (source, target) in enumerate(
            ((ids_hbm, ids), (gates_hbm, gates), (inputs_hbm, inputs), (grads_hbm, grads))
        )
    ]
    for load in loads:
        load.start()
    tokens = ids.shape[1]
    padded = max(8, experts)
    group = lax.div(lax.axis_index("expert"), HSPLIT)
    earlier = (iota((tokens, tokens), 0) < iota((tokens, tokens), 1)).astype(F32).astype(BF16)
    loads[0].wait()
    loads[1].wait()
    expert_ids = ids[...]
    route_gates = gates[...]
    match_rows = jnp.zeros((padded, tokens), F32)
    matches = []
    token_gates = []
    for step in range(experts):
        hits = expert_ids == lax.rem(group + step, experts)
        match = jnp.sum(hits.astype(F32), axis=0, keepdims=True)
        matches.append(match)
        token_gates.append(jnp.sum(jnp.where(hits, route_gates, 0.0), axis=0, keepdims=True))
        match_rows = jnp.where(iota((padded, tokens), 0) == step, match, match_rows)
    counts = dot(match_rows.astype(BF16), earlier)
    slots = [
        jnp.where(matches[step] > 0.0, counts[step : step + 1, :], -1.0e6)
        for step in range(experts)
    ]

    def chosen(rows, offset):
        places = (iota((rows, tokens), 0) - offset).astype(F32)
        return [(places == slots[step]).astype(F32) for step in range(experts)]

    input_picks = chosen(2 * CAP, 0)
    grad_picks = chosen(2 * CAP, CAP)
    slot_gates = [
        jnp.sum(hit * gate, axis=1, keepdims=True) for hit, gate in zip(grad_picks, token_gates)
    ]
    gate_column = jnp.concatenate(slot_gates, axis=0)
    input_picks = jnp.concatenate(input_picks, axis=0)
    grad_picks = jnp.concatenate(grad_picks, axis=0)
    if fold == 2:
        picks[0][...] = input_picks.astype(BF16)
        picks[1][...] = grad_picks.astype(BF16)
    else:
        picks[0][...] = jnp.concatenate(chosen(CAP, 0), axis=0).astype(BF16)
    loads[2].wait()
    total = dot(input_picks.astype(BF16), inputs[...])
    loads[3].wait()
    total = total + dot(grad_picks.astype(BF16), grads[...]) * gate_column
    for step in range(experts):
        pieces[step][...] = total[step * 2 * CAP : (step + 1) * 2 * CAP].astype(BF16)


def load_body(after, *refs):
    count = len(refs) // 2
    sems = refs[-1]
    loads = [
        pltpu.make_async_copy(refs[place], refs[count + place], sems.at[place])
        for place in range(count)
    ]
    for load in loads:
        load.start()
    for load in loads:
        load.wait()


def take_rows(offset, pieces, stack):
    place = 0
    for ref in pieces:
        stack[place : place + ref.shape[0], :] = ref[...].astype(F32)
        place += ref.shape[0]
    count = place // 2
    rows = iota((count, place), 0)
    mover = iota((count, place), 1) == rows + over_cap(rows) * CAP + offset
    return dot(mover.astype(F32).astype(BF16), stack[...].astype(BF16)).astype(BF16)


def forward_body(w_gate, w_up, *refs):
    pieces, (rows_out, keep, send, stack) = refs[:-4], refs[-4:]
    half = w_gate.shape[1] // 2
    rows = take_rows(0, pieces, stack)
    rows_out[...] = rows
    for target, far in ((send, True), (keep, False)):
        columns = core_columns(half, far)
        target[:, :half] = dot(rows, w_gate[:, columns]).astype(BF16)
        target[:, half:] = dot(rows, w_up[:, columns]).astype(BF16)


def hidden_body(w_down, *refs):
    pieces, (keep, send, stack) = refs[:-3], refs[-3:]
    half = w_down.shape[0] // 2
    rows = take_rows(CAP, pieces, stack)
    for target, far in ((send, True), (keep, False)):
        target[...] = dot(rows, w_down[core_columns(half, far), :], 1, 1).astype(BF16)


def activate_body(pre_own, pre_far, hid_own, hid_far, acts):
    half = hid_own.shape[1]
    pre = pre_own[...].astype(F32) + pre_far[...].astype(F32)
    hidden_grad = hid_own[...].astype(F32) + hid_far[...].astype(F32)
    gate_pre = pre[:, :half]
    up_pre = pre[:, half:]
    sigma = jax.nn.sigmoid(gate_pre)
    acts[:, :half] = (hidden_grad * up_pre * sigma * (1.0 + gate_pre * (1.0 - sigma))).astype(BF16)
    acts[:, half:] = (hidden_grad * gate_pre * sigma).astype(BF16)


def back_part(w_gate, w_up, acts, far):
    half = w_gate.shape[1] // 2
    columns = core_columns(half, far)
    part = dot(acts[:, :half], w_gate[:, columns], 1, 1)
    return part + dot(acts[:, half:], w_up[:, columns], 1, 1)


def back_own_body(w_gate, w_up, acts, total):
    total[...] = back_part(w_gate, w_up, acts, False)


def back_far_body(w_gate, w_up, acts, own, *outs):
    count = outs[0].shape[0]
    total = own[...] + back_part(w_gate, w_up, acts, True)
    for place, out in enumerate(outs):
        out[...] = total[place * count : (place + 1) * count].astype(BF16)


def weight_body(which, chunks, after, rows_ref, acts_own, acts_far, out, token, tile, sems):
    token[...] = jnp.zeros_like(token)
    half = out.shape[1] // 2
    depth = out.shape[0] // chunks
    stores = []
    for chunk in range(chunks):
        span = slice(chunk * depth, (chunk + 1) * depth)
        rows = rows_ref[:, span]
        for acts, far in ((acts_own, False), (acts_far, True)):
            part = dot(rows, acts[:, which * half : (which + 1) * half], 0, 0)
            tile[span, core_columns(half, far)] = part.astype(BF16)
        stores.append(pltpu.make_async_copy(tile.at[span], out.at[span], sems.at[chunk]))
        stores[-1].start()
    for store in stores:
        store.wait()


def gather_body(fold, experts, after, own, one, two, three, *outs):
    total = own[...].astype(F32) + one[...].astype(F32)
    total = (total + (two[...].astype(F32) + three[...].astype(F32))).astype(BF16)
    count = total.shape[0]
    width = total.shape[1] // fold
    piece = CAP * fold
    rows = iota((fold * count, count), 1)
    folded = None
    for part in range(fold):
        goal = rows + over_cap(rows) * (CAP * (fold - 1)) + part * CAP
        mover = (iota((fold * count, count), 0) == goal).astype(F32).astype(BF16)
        moved = dot(mover, total[:, part * width : (part + 1) * width])
        folded = moved if folded is None else folded + moved
    for step in range(experts):
        outs[step][...] = folded[step * piece : (step + 1) * piece].astype(BF16)


def scatter_body(fold, experts, *refs):
    picks, pieces = refs[:fold], refs[fold : fold + experts]
    out, stack, tile, sems = refs[-4:]
    width = out.shape[1] // fold
    piece = CAP * fold
    for step in range(experts):
        stack[step * piece : (step + 1) * piece, :] = pieces[step][...].astype(F32)
    returned = stack[...].astype(BF16)
    stores = []
    for part in range(fold):
        span = slice(part * width, (part + 1) * width)
        tile[:, span] = dot(picks[part][...], returned, 0, 0).astype(BF16)
        stores.append(pltpu.make_async_copy(tile.at[:, span], out.at[:, span], sems.at[part]))
        stores[-1].start()
    for store in stores:
        store.wait()


def per_device(out_grad, inputs, expert_ids, gate_weights, w_gate, w_up, w_down):
    devices = lax.axis_size("expert")
    spread = lax.axis_size("dp")
    experts = devices // HSPLIT
    tokens, features = out_grad.shape
    routed = expert_ids.shape[1]
    fold = fold_of(features)
    hidden = w_gate.shape[1]
    half = hidden // 2
    count = devices * CAP
    product = 2 * count * features * hidden
    dma = pltpu.SemaphoreType.DMA

    def to_expert(value, step):
        pairs = [(d, (d + step * HSPLIT) % devices) for d in range(devices)]
        return lax.ppermute(value, "expert", pairs)

    def to_peer(value, flip):
        return lax.ppermute(value, "expert", [(d, d ^ flip) for d in range(devices)])

    def to_dp(value, flip):
        return lax.ppermute(value, "dp", [(d, d ^ flip) for d in range(spread)])

    picked = run(
        functools.partial(pick_body, experts, fold),
        (shape((experts * fold * CAP, tokens)),) * fold
        + (shape((2 * CAP, features)),) * experts,
        [HBM] * 4,
        8 * experts * CAP * tokens * features,
        4 * tokens * features,
        *(in_hbm(array) for array in (expert_ids.T, gate_weights.T, out_grad, inputs)),
        scratch=(
            pltpu.VMEM((routed, tokens), jnp.int32),
            pltpu.VMEM((routed, tokens), F32),
            pltpu.VMEM((tokens, features), BF16),
            pltpu.VMEM((tokens, features), BF16),
            dma((4,)),
        ),
    )
    picks, own = picked[:fold], picked[fold:]
    weights = (w_gate, w_up, w_down)
    gate_here, up_here, down_here = run(
        load_body,
        tuple(pltpu.VMEM(weight.shape, weight.dtype) for weight in weights),
        [ANY] + [HBM] * 3,
        0,
        6 * features * hidden,
        picks[0],
        *(in_hbm(weight) for weight in weights),
        scratch=(dma((3,)),),
    )

    away = [to_expert(own[step], step) for step in range(1, experts)]
    pieces = [own[0]] + [to_peer(own[0], flip) for flip in range(1, HSPLIT)]
    if away:
        away = away[0] if len(away) == 1 else jnp.concatenate(away, axis=0)
        others = [away] + [to_peer(away, flip) for flip in range(1, HSPLIT)]
        pieces = [array for pair in zip(pieces, others) for array in pair]

    stack = pltpu.VMEM((2 * count, features), F32)
    rows_input, pre_keep, pre_send = run(
        forward_body,
        (shape((count, features)), shape((count, hidden)), shape((count, hidden))),
        [VMEM] * (2 + len(pieces)),
        2 * product,
        4 * features * hidden,
        gate_here,
        up_here,
        *pieces,
        scratch=(stack,),
    )

    def spread_sum(keep, send):
        near = (keep.astype(F32) + to_dp(send, 1).astype(F32)).astype(BF16)
        flip = 2
        far = jnp.zeros_like(near)
        while flip < spread:
            far = to_dp(near, flip)
            flip *= 2
            if flip < spread:
                near = (near.astype(F32) + far.astype(F32)).astype(BF16)
        return near, far

    pre_own, pre_far = spread_sum(pre_keep, pre_send)
    hid_keep, hid_send = run(
        hidden_body,
        (shape((count, half)), shape((count, half))),
        [VMEM] * (1 + len(pieces)),
        product,
        2 * features * hidden,
        down_here,
        *pieces,
        scratch=(stack,),
    )
    hid_own, hid_far = spread_sum(hid_keep, hid_send)
    acts = run(
        activate_body,
        shape((count, hidden)),
        [VMEM] * 4,
        20 * count * half,
        10 * count * half,
        pre_own,
        pre_far,
        hid_own,
        hid_far,
    )
    acts_far = to_dp(acts, 1)
    back_own = run(
        back_own_body,
        shape((count, features), F32),
        [VMEM] * 3,
        product,
        2 * features * hidden,
        gate_here,
        up_here,
        acts,
    )
    back = run(
        back_far_body,
        (shape((count // HSPLIT, features)),) * HSPLIT,
        [VMEM] * 4,
        product,
        2 * features * hidden,
        gate_here,
        up_here,
        acts_far,
        back_own,
    )
    back_far = [to_peer(back[flip], flip) for flip in range(1, HSPLIT)]

    def weight_grad(which, after):
        chunks = 2
        return run(
            functools.partial(weight_body, which, chunks),
            (shape((features, hidden)), shape((8, 128), F32)),
            [ANY] + [VMEM] * 3,
            product,
            4 * features * hidden,
            after,
            rows_input,
            acts,
            acts_far,
            out_spec=(HBM, VMEM),
            scratch=(pltpu.VMEM((features, hidden), BF16), dma((chunks,))),
        )

    grad_gate, token = weight_grad(0, back[0])
    summed = run(
        functools.partial(gather_body, fold, experts),
        (shape((CAP * fold, features // fold)),) * experts,
        [ANY] + [VMEM] * HSPLIT,
        4 * count * features,
        4 * count * features,
        token,
        back[0],
        *back_far,
    )
    grad_up, _ = weight_grad(1, summed[0])
    returned = [summed[0]] + [to_expert(summed[step], experts - step) for step in range(1, experts)]
    in_grad = run(
        functools.partial(scatter_body, fold, experts),
        shape((tokens, features)),
        [VMEM] * (fold + experts),
        4 * experts * CAP * tokens * features,
        2 * tokens * features,
        *picks,
        *returned,
        out_spec=HBM,
        scratch=(
            pltpu.VMEM((experts * fold * CAP, features // fold), F32),
            pltpu.VMEM((tokens, features), BF16),
            dma((fold,)),
        ),
    )
    return (in_grad, grad_gate, grad_up)


def solution(mesh):
    placed = (
        P("expert", "dp"),
        P("expert", "dp"),
        P("expert", None),
        P("expert", None),
        P("dp", "expert"),
        P("dp", "expert"),
        P("expert", "dp"),
    )
    return jax.shard_map(
        per_device,
        mesh=mesh,
        in_specs=placed,
        out_specs=(P("expert", "dp"), P("dp", "expert"), P("dp", "expert")),
        check_vma=False,
    )
```

```python
import functools

import jax
import jax.numpy as jnp
from jax import lax
from jax.experimental import pallas as pl
from jax.experimental.pallas import tpu as pltpu
from jax.sharding import PartitionSpec as P

HSPLIT = 4
CAP = 12
F32 = jnp.float32
BF16 = jnp.bfloat16
VMEM = pl.BlockSpec(memory_space=pltpu.VMEM)
HBM = pl.BlockSpec(memory_space=pltpu.HBM)
ANY = pl.BlockSpec(memory_space=pl.ANY)


NEAR_ORDER = (1, 3, 0, 2)
FAR_ORDER = (3, 2, 1, 0)


def shape(dims, dtype=BF16):
    return jax.ShapeDtypeStruct(dims, dtype)


def run(body, outs, specs, flops, nbytes, *args, out_spec=VMEM, scratch=()):
    return pl.pallas_call(
        body,
        out_shape=outs,
        in_specs=specs,
        out_specs=out_spec if isinstance(out_spec, tuple) else jax.tree.map(lambda _: out_spec, outs),
        scratch_shapes=scratch,
        compiler_params=pltpu.CompilerParams(vmem_limit_bytes=40 * 1024 * 1024),
        cost_estimate=pl.CostEstimate(flops=flops, bytes_accessed=nbytes, transcendentals=0),
    )(*args)


def in_hbm(value):
    return pltpu.with_memory_space_constraint(value, pltpu.HBM)


def dot(left, right, left_dim=1, right_dim=0):
    return lax.dot_general(
        left, right, (((left_dim,), (right_dim,)), ((), ())), preferred_element_type=F32
    )


def iota(dims, dim):
    return lax.broadcasted_iota(jnp.int32, dims, dim)


def over_cap(rows):
    return jnp.floor((rows.astype(F32) + 0.5) * (1.0 / CAP)).astype(jnp.int32)


def column_spans(width):
    whole = width // 128 * 128
    if whole != width or width < 512:
        return [slice(0, width)]
    middle = width // 256 * 128
    return [slice(0, middle), slice(middle, width)]


def core_columns(width, far):
    side = lax.rem(lax.axis_index("dp"), 2)
    side = 1 - side if far else side
    return pl.ds(pl.multiple_of(side * width, width), width)


def fold_of(width):
    return 2 if width % 256 == 0 else 1


def pick_body(experts, fold, ids_hbm, gates_hbm, grads_hbm, inputs_hbm, *refs):
    picks, pieces = refs[:fold], refs[fold : fold + experts]
    ids, gates, grads, inputs, sems = refs[fold + experts :]
    spans = column_spans(grads.shape[1])
    moves = [(ids_hbm, ids), (gates_hbm, gates)]
    for span in spans:
        moves.append((inputs_hbm.at[:, span], inputs.at[:, span]))
        moves.append((grads_hbm.at[:, span], grads.at[:, span]))
    loads = [
        pltpu.make_async_copy(source, target, sems.at[place])
        for place, (source, target) in enumerate(moves)
    ]
    for load in loads:
        load.start()
    tokens = ids.shape[1]
    padded = max(8, experts)
    group = lax.div(lax.axis_index("expert"), HSPLIT)
    earlier = (iota((tokens, tokens), 0) < iota((tokens, tokens), 1)).astype(F32).astype(BF16)
    loads[0].wait()
    loads[1].wait()
    expert_ids = ids[...]
    route_gates = gates[...]
    match_rows = jnp.zeros((padded, tokens), F32)
    matches = []
    token_gates = []
    for step in range(experts):
        hits = expert_ids == lax.rem(group + step, experts)
        match = jnp.sum(hits.astype(F32), axis=0, keepdims=True)
        matches.append(match)
        token_gates.append(jnp.sum(jnp.where(hits, route_gates, 0.0), axis=0, keepdims=True))
        match_rows = jnp.where(iota((padded, tokens), 0) == step, match, match_rows)
    counts = dot(match_rows.astype(BF16), earlier)
    slots = [
        jnp.where(matches[step] > 0.0, counts[step : step + 1, :], -1.0e6)
        for step in range(experts)
    ]

    def chosen(rows, offset):
        places = (iota((rows, tokens), 0) - offset).astype(F32)
        return [(places == slots[step]).astype(F32) for step in range(experts)]

    input_picks = chosen(2 * CAP, 0)
    grad_picks = chosen(2 * CAP, CAP)
    slot_gates = [
        jnp.sum(hit * gate, axis=1, keepdims=True) for hit, gate in zip(grad_picks, token_gates)
    ]
    gate_column = jnp.concatenate(slot_gates, axis=0)
    input_picks = jnp.concatenate(input_picks, axis=0)
    grad_picks = jnp.concatenate(grad_picks, axis=0)
    if fold == 2:
        picks[0][...] = input_picks.astype(BF16)
        picks[1][...] = grad_picks.astype(BF16)
    else:
        picks[0][...] = jnp.concatenate(chosen(CAP, 0), axis=0).astype(BF16)
    input_picks = input_picks.astype(BF16)
    grad_picks = grad_picks.astype(BF16)
    for place, span in enumerate(spans):
        loads[2 + 2 * place].wait()
        total = dot(input_picks, inputs[:, span])
        loads[3 + 2 * place].wait()
        total = total + dot(grad_picks, grads[:, span]) * gate_column
        for step in range(experts):
            rows = slice(step * 2 * CAP, (step + 1) * 2 * CAP)
            pieces[step][:, span] = total[rows].astype(BF16)


def take_rows(pieces, stack):
    place = 0
    for ref in pieces:
        stack[place : place + ref.shape[0], :] = ref[...].astype(F32)
        place += ref.shape[0]
    stacked = stack[...].astype(BF16)
    count = place // 2
    rows = iota((count, place), 0)
    source = rows + over_cap(rows) * CAP
    taken = []
    for offset in (0, CAP):
        mover = (iota((count, place), 1) == source + offset).astype(F32).astype(BF16)
        taken.append(dot(mover, stacked).astype(BF16))
    return taken


def pre_part(rows, weight, place, keep, send):
    half = weight.shape[1] // 2
    span = slice(place * half, (place + 1) * half)
    for target, far in ((send, True), (keep, False)):
        target[:, span] = dot(rows, weight[:, core_columns(half, far)]).astype(BF16)


def hidden_part(rows, weight, keep, send):
    half = weight.shape[0] // 2
    for target, far in ((send, True), (keep, False)):
        part = dot(rows, weight[core_columns(half, far), :], 1, 1)
        target[:, 2 * half :] = part.astype(BF16)


def near_body(after, w_gate, up_hbm, down_hbm, *refs):
    pieces = refs[:-7]
    w_up, w_down, rows_out, keep, send, stack, sems = refs[-7:]
    load_up = pltpu.make_async_copy(up_hbm, w_up, sems.at[0])
    load_down = pltpu.make_async_copy(down_hbm, w_down, sems.at[1])
    load_up.start()
    load_down.start()
    input_rows, grad_rows = take_rows(pieces, stack)
    rows_out[...] = input_rows
    pre_part(input_rows, w_gate, 0, keep, send)
    load_up.wait()
    pre_part(input_rows, w_up, 1, keep, send)
    load_down.wait()
    hidden_part(grad_rows, w_down, keep, send)


def far_body(w_gate, w_up, w_down, *refs):
    pieces = refs[:-4]
    rows_out, keep, send, stack = refs[-4:]
    input_rows, grad_rows = take_rows(pieces, stack)
    rows_out[...] = input_rows
    pre_part(input_rows, w_gate, 0, keep, send)
    pre_part(input_rows, w_up, 1, keep, send)
    hidden_part(grad_rows, w_down, keep, send)


def core_sum_body(own, other, *refs):
    refs[-1][...] = (own[...].astype(F32) + other[...].astype(F32)).astype(BF16)


def activate_body(own, other, *refs):
    acts = refs[-1]
    half = own.shape[1] // 3
    total = own[...].astype(F32) + other[...].astype(F32)
    gate_pre = total[:, :half]
    up_pre = total[:, half : 2 * half]
    hidden_grad = total[:, 2 * half :]
    sigma = jax.nn.sigmoid(gate_pre)
    acts[:, :half] = (hidden_grad * up_pre * sigma * (1.0 + gate_pre * (1.0 - sigma))).astype(BF16)
    acts[:, half:] = (hidden_grad * gate_pre * sigma).astype(BF16)


def fold_rows(total, fold):
    count = total.shape[0]
    width = total.shape[1] // fold
    rows = iota((fold * count, count), 1)
    folded = None
    for part in range(fold):
        goal = rows + over_cap(rows) * (CAP * (fold - 1)) + part * CAP
        mover = (iota((fold * count, count), 0) == goal).astype(F32).astype(BF16)
        moved = dot(mover, total[:, part * width : (part + 1) * width])
        folded = moved if folded is None else folded + moved
    return folded.astype(BF16)


def back_part(w_gate, w_up, acts, sibling):
    half = w_gate.shape[1] // 2
    columns = core_columns(half, sibling)
    part = dot(acts[:, :half], w_gate[:, columns], 1, 1)
    return part + dot(acts[:, half:], w_up[:, columns], 1, 1)


def back_own_body(w_gate, w_up, near, far, near_total, far_total):
    count = near.shape[0]
    acts = jnp.concatenate([near[...], far[...]], axis=0)
    total = back_part(w_gate, w_up, acts, False)
    near_total[...] = total[:count]
    far_total[...] = total[count:]


def back_far_body(fold, w_gate, w_up, far, own, *outs):
    total = (own[...] + back_part(w_gate, w_up, far[...], True)).astype(BF16)
    folded = fold_rows(total, fold)
    count = outs[0].shape[0]
    for place, out in enumerate(outs):
        out[...] = folded[place * count : (place + 1) * count]


def back_near_body(after, w_gate, w_up, near, own, send, keep):
    total = (own[...] + back_part(w_gate, w_up, near[...], True)).astype(BF16)
    count = send.shape[0]
    send[...] = total[:count]
    keep[...] = total[count:]


def weight_body(which, chunks, after, *refs):
    rows_near, rows_far, own_near, own_far, sib_near, sib_far = refs[:6]
    out, token, tile, rows_all, sems = refs[6:]
    token[...] = jnp.zeros_like(token)
    half = out.shape[1] // 2
    depth = out.shape[0] // chunks
    split = rows_near.shape[0]
    rows_all[:split, :] = rows_near[...]
    rows_all[split:, :] = rows_far[...]
    span = slice(which * half, (which + 1) * half)
    own = jnp.concatenate([own_near[:, span], own_far[:, span]], axis=0)
    sib = jnp.concatenate([sib_near[:, span], sib_far[:, span]], axis=0)
    stores = []
    for chunk in range(chunks):
        span = slice(chunk * depth, (chunk + 1) * depth)
        rows = rows_all[:, span]
        for acts, far in ((own, False), (sib, True)):
            tile[span, core_columns(half, far)] = dot(rows, acts, 0, 0).astype(BF16)
        stores.append(pltpu.make_async_copy(tile.at[span], out.at[span], sems.at[chunk]))
        stores[-1].start()
    for store in stores:
        store.wait()


def near_sum_body(fold, after, own, other, keep, send):
    total = (own[...].astype(F32) + other[...].astype(F32)).astype(BF16)
    folded = fold_rows(total, fold)
    keep[...] = folded[: keep.shape[0]]
    send[...] = folded[keep.shape[0] :]


def far_sum_body(after, own, one, two, three, *outs):
    total = own[...].astype(F32) + one[...].astype(F32)
    total = total + (two[...].astype(F32) + three[...].astype(F32))
    count = outs[0].shape[0]
    for place, out in enumerate(outs):
        out[...] = total[place * count : (place + 1) * count].astype(BF16)


def scatter_body(fold, *refs):
    picks, (near_own, near_other), pieces = refs[:fold], refs[fold : fold + 2], refs[fold + 2 : -4]
    out, stack, tile, sems = refs[-4:]
    width = out.shape[1] // fold
    piece = CAP * fold
    stack[:piece, :] = near_own[...].astype(F32) + near_other[...].astype(F32)
    for place, ref in enumerate(pieces):
        stack[(place + 1) * piece : (place + 2) * piece, :] = ref[...].astype(F32)
    returned = stack[...].astype(BF16)
    stores = []
    for part in range(fold):
        for span in column_spans(width):
            target = slice(part * width + span.start, part * width + span.stop)
            tile[:, target] = dot(picks[part][...], returned[:, span], 0, 0).astype(BF16)
            store = pltpu.make_async_copy(
                tile.at[:, target], out.at[:, target], sems.at[len(stores)]
            )
            store.start()
            stores.append(store)
    for store in stores:
        store.wait()


def per_device(out_grad, inputs, expert_ids, gate_weights, w_gate, w_up, w_down):
    devices = lax.axis_size("expert")
    spread = lax.axis_size("dp")
    experts = devices // HSPLIT
    tokens, features = out_grad.shape
    routed = expert_ids.shape[1]
    fold = fold_of(features)
    hidden = w_gate.shape[1]
    half = hidden // 2
    count = devices * CAP
    product = 2 * count * features * hidden
    dma = pltpu.SemaphoreType.DMA

    def to_expert(value, step):
        pairs = [(d, (d + step * HSPLIT) % devices) for d in range(devices)]
        return lax.ppermute(value, "expert", pairs)

    def to_peer(value, flip):
        return lax.ppermute(value, "expert", [(d, d ^ flip) for d in range(devices)])

    def to_dp(value, flip):
        return lax.ppermute(value, "dp", [(d, d ^ flip) for d in range(spread)])

    picked = run(
        functools.partial(pick_body, experts, fold),
        (shape((experts * fold * CAP, tokens)),) * fold
        + (shape((2 * CAP, features)),) * experts,
        [HBM] * 4,
        8 * experts * CAP * tokens * features,
        4 * tokens * features,
        *(in_hbm(array) for array in (expert_ids.T, gate_weights.T, out_grad, inputs)),
        scratch=(
            pltpu.VMEM((routed, tokens), jnp.int32),
            pltpu.VMEM((routed, tokens), F32),
            pltpu.VMEM((tokens, features), BF16),
            pltpu.VMEM((tokens, features), BF16),
            dma((2 + 2 * len(column_spans(features)),)),
        ),
    )
    picks, own = picked[:fold], picked[fold:]
    away = [to_expert(own[step], step) for step in range(1, experts)]
    near = [own[0]] + [to_peer(own[0], flip) for flip in range(1, HSPLIT)]
    away = away[0] if len(away) == 1 else jnp.concatenate(away, axis=0)
    far = [away] + [to_peer(away, flip) for flip in range(1, HSPLIT)]

    def rows_shapes(rows):
        return (shape((rows, features)), shape((rows, 3 * half)), shape((rows, 3 * half)))

    near_count = HSPLIT * CAP
    far_count = count - near_count
    up_here, down_here, rows_near, near_pre, near_send = run(
        near_body,
        tuple(pltpu.VMEM(weight.shape, weight.dtype) for weight in (w_up, w_down))
        + rows_shapes(near_count),
        [ANY, VMEM] + [HBM] * 2 + [VMEM] * HSPLIT,
        3 * product,
        6 * features * hidden,
        away,
        w_gate,
        in_hbm(w_up),
        in_hbm(w_down),
        *(near[peer] for peer in NEAR_ORDER),
        scratch=(pltpu.VMEM((2 * near_count, features), F32), dma((2,))),
    )
    rows_far, far_pre, far_send = run(
        far_body,
        rows_shapes(far_count),
        [VMEM] * (3 + HSPLIT),
        3 * product // 2,
        6 * features * hidden,
        w_gate,
        up_here,
        down_here,
        *(far[peer] for peer in FAR_ORDER),
        scratch=(pltpu.VMEM((2 * far_count, features), F32),),
    )

    def core_sum(keep, send, *after):
        return run(
            core_sum_body,
            shape(keep.shape),
            [VMEM] * 2 + [ANY] * len(after),
            0,
            0,
            keep,
            to_dp(send, 1),
            *after,
        )

    def activate(total, *after):
        flip = 2
        other = jnp.zeros_like(total)
        while flip < spread:
            other = to_dp(total, flip)
            flip *= 2
            if flip < spread:
                total = (total.astype(F32) + other.astype(F32)).astype(BF16)
        rows = total.shape[0]
        return run(
            activate_body,
            shape((rows, hidden)),
            [VMEM] * 2 + [ANY] * len(after),
            20 * rows * half,
            10 * rows * half,
            total,
            other,
            *after,
        )

    near_total = core_sum(near_pre, near_send)
    far_total = core_sum(far_pre, far_send, near_total)
    acts_near = activate(near_total)
    acts_far = activate(far_total, acts_near)
    sib_near = to_dp(acts_near, 1)
    sib_far = to_dp(acts_far, 1)
    near_total, far_total = run(
        back_own_body,
        (shape((near_count, features), F32), shape((far_count, features), F32)),
        [VMEM] * 4,
        product,
        2 * features * hidden,
        w_gate,
        up_here,
        acts_near,
        acts_far,
    )
    far_rows = shape((far_count // HSPLIT * fold, features // fold))
    far_out = run(
        functools.partial(back_far_body, fold),
        (far_rows,) * HSPLIT,
        [VMEM] * 4,
        product,
        2 * features * hidden,
        w_gate,
        up_here,
        sib_far,
        far_total,
    )
    near_out, near_keep = run(
        back_near_body,
        (shape((2 * CAP, features)),) * 2,
        [ANY] + [VMEM] * 4,
        product,
        2 * features * hidden,
        far_out[-1],
        w_gate,
        up_here,
        sib_near,
        near_total,
    )

    def weight_grad(which, after):
        chunks = 4 if features % 512 == 0 else 2
        return run(
            functools.partial(weight_body, which, chunks),
            (shape((features, hidden)), shape((8, 128), F32)),
            [ANY] + [VMEM] * 6,
            0,
            0,
            after,
            rows_near,
            rows_far,
            acts_near,
            acts_far,
            sib_near,
            sib_far,
            out_spec=(HBM, VMEM),
            scratch=(
                pltpu.VMEM((features, hidden), BF16),
                pltpu.VMEM((count, features), BF16),
                dma((chunks,)),
            ),
        )

    grad_gate, token = weight_grad(0, far_out[-1])
    piece = shape((CAP * fold, features // fold))
    summed = run(
        far_sum_body,
        (piece,) * (experts - 1),
        [ANY] + [VMEM] * HSPLIT,
        4 * product,
        0,
        token,
        *(to_peer(out, peer) for out, peer in zip(far_out, FAR_ORDER) if peer),
        far_out[FAR_ORDER.index(0)],
    )
    near_own, near_last = run(
        functools.partial(near_sum_body, fold),
        (piece,) * 2,
        [ANY] + [VMEM] * 2,
        0,
        0,
        summed[0],
        near_keep,
        to_peer(near_out, 1),
    )
    near_other = to_peer(near_last, 2)
    grad_up, _ = weight_grad(1, near_last)
    returned = [to_expert(summed[step - 1], experts - step) for step in range(1, experts)]
    in_grad = run(
        functools.partial(scatter_body, fold),
        shape((tokens, features)),
        [VMEM] * (fold + 2 + len(returned)),
        4 * experts * CAP * tokens * features,
        2 * tokens * features,
        *picks,
        near_own,
        near_other,
        *returned,
        out_spec=HBM,
        scratch=(
            pltpu.VMEM((experts * fold * CAP, features // fold), F32),
            pltpu.VMEM((tokens, features), BF16),
            dma((fold * len(column_spans(features // fold)),)),
        ),
    )
    return (in_grad, grad_gate, grad_up)


def solution(mesh):
    placed = (
        P("expert", "dp"),
        P("expert", "dp"),
        P("expert", None),
        P("expert", None),
        P("dp", "expert"),
        P("dp", "expert"),
        P("expert", "dp"),
    )
    return jax.shard_map(
        per_device,
        mesh=mesh,
        in_specs=placed,
        out_specs=(P("expert", "dp"), P("dp", "expert"), P("dp", "expert")),
        check_vma=False,
    )
```

```python
import functools

import jax
import jax.numpy as jnp
from jax import lax
from jax.experimental import pallas as pl
from jax.experimental.pallas import tpu as pltpu
from jax.sharding import PartitionSpec as P

HSPLIT = 4
CAP = 12
F32 = jnp.float32
BF16 = jnp.bfloat16
VMEM = pl.BlockSpec(memory_space=pltpu.VMEM)
HBM = pl.BlockSpec(memory_space=pltpu.HBM)
ANY = pl.BlockSpec(memory_space=pl.ANY)


def shape(dims, dtype=BF16):
    return jax.ShapeDtypeStruct(dims, dtype)


def run(body, outs, specs, flops, nbytes, *args, out_spec=VMEM, scratch=()):
    return pl.pallas_call(
        body,
        out_shape=outs,
        in_specs=specs,
        out_specs=out_spec if isinstance(out_spec, tuple) else jax.tree.map(lambda _: out_spec, outs),
        scratch_shapes=scratch,
        compiler_params=pltpu.CompilerParams(vmem_limit_bytes=40 * 1024 * 1024),
        cost_estimate=pl.CostEstimate(flops=flops, bytes_accessed=nbytes, transcendentals=0),
    )(*args)


def in_hbm(value):
    return pltpu.with_memory_space_constraint(value, pltpu.HBM)


def dot(left, right, left_dim=1, right_dim=0):
    return lax.dot_general(
        left, right, (((left_dim,), (right_dim,)), ((), ())), preferred_element_type=F32
    )


def iota(dims, dim):
    return lax.broadcasted_iota(jnp.int32, dims, dim)


def over_cap(rows):
    return jnp.floor((rows.astype(F32) + 0.5) * (1.0 / CAP)).astype(jnp.int32)


def column_spans(width):
    whole = width // 128 * 128
    if whole != width or width < 512:
        return [slice(0, width)]
    middle = width // 256 * 128
    return [slice(0, middle), slice(middle, width)]


def core_columns(width, far):
    side = lax.rem(lax.axis_index("dp"), 2)
    side = 1 - side if far else side
    return pl.ds(pl.multiple_of(side * width, width), width)


def fold_of(width):
    return 2 if width % 256 == 0 else 1


def pick_body(experts, fold, ids_hbm, gates_hbm, grads_hbm, inputs_hbm, *refs):
    picks, pieces = refs[:fold], refs[fold : fold + experts]
    ids, gates, grads, inputs, sems = refs[fold + experts :]
    spans = column_spans(grads.shape[1])
    moves = [(ids_hbm, ids), (gates_hbm, gates)]
    for span in spans:
        moves.append((inputs_hbm.at[:, span], inputs.at[:, span]))
        moves.append((grads_hbm.at[:, span], grads.at[:, span]))
    loads = [
        pltpu.make_async_copy(source, target, sems.at[place])
        for place, (source, target) in enumerate(moves)
    ]
    for load in loads:
        load.start()
    tokens = ids.shape[1]
    padded = max(8, experts)
    group = lax.div(lax.axis_index("expert"), HSPLIT)
    earlier = (iota((tokens, tokens), 0) < iota((tokens, tokens), 1)).astype(F32).astype(BF16)
    loads[0].wait()
    loads[1].wait()
    expert_ids = ids[...]
    route_gates = gates[...]
    match_rows = jnp.zeros((padded, tokens), F32)
    matches = []
    token_gates = []
    for step in range(experts):
        hits = expert_ids == lax.rem(group + step, experts)
        match = jnp.sum(hits.astype(F32), axis=0, keepdims=True)
        matches.append(match)
        token_gates.append(jnp.sum(jnp.where(hits, route_gates, 0.0), axis=0, keepdims=True))
        match_rows = jnp.where(iota((padded, tokens), 0) == step, match, match_rows)
    counts = dot(match_rows.astype(BF16), earlier)
    slots = [
        jnp.where(matches[step] > 0.0, counts[step : step + 1, :], -1.0e6)
        for step in range(experts)
    ]

    def chosen(rows, offset):
        places = (iota((rows, tokens), 0) - offset).astype(F32)
        return [(places == slots[step]).astype(F32) for step in range(experts)]

    input_picks = chosen(2 * CAP, 0)
    grad_picks = chosen(2 * CAP, CAP)
    slot_gates = [
        jnp.sum(hit * gate, axis=1, keepdims=True) for hit, gate in zip(grad_picks, token_gates)
    ]
    gate_column = jnp.concatenate(slot_gates, axis=0)
    input_picks = jnp.concatenate(input_picks, axis=0)
    grad_picks = jnp.concatenate(grad_picks, axis=0)
    if fold == 2:
        picks[0][...] = input_picks.astype(BF16)
        picks[1][...] = grad_picks.astype(BF16)
    else:
        picks[0][...] = jnp.concatenate(chosen(CAP, 0), axis=0).astype(BF16)
    input_picks = input_picks.astype(BF16)
    grad_picks = grad_picks.astype(BF16)
    for place, span in enumerate(spans):
        loads[2 + 2 * place].wait()
        total = dot(input_picks, inputs[:, span])
        loads[3 + 2 * place].wait()
        total = total + dot(grad_picks, grads[:, span]) * gate_column
        for step in range(experts):
            rows = slice(step * 2 * CAP, (step + 1) * 2 * CAP)
            pieces[step][:, span] = total[rows].astype(BF16)


def load_body(parts, after, *refs):
    count = len(refs) // 2
    sems = refs[-1]
    loads = []
    for place in range(count):
        depth = refs[place].shape[0] // parts
        for part in range(parts):
            rows = slice(part * depth, (part + 1) * depth)
            source, target = refs[place].at[rows], refs[count + place].at[rows]
            loads.append(pltpu.make_async_copy(source, target, sems.at[len(loads)]))
    for load in loads:
        load.start()
    for load in loads:
        load.wait()


def take_rows(offset, pieces, stack):
    place = 0
    for ref in pieces:
        stack[place : place + ref.shape[0], :] = ref[...].astype(F32)
        place += ref.shape[0]
    count = place // 2
    rows = iota((count, place), 0)
    mover = iota((count, place), 1) == rows + over_cap(rows) * CAP + offset
    return dot(mover.astype(F32).astype(BF16), stack[...].astype(BF16)).astype(BF16)


def forward_body(w_gate, w_up, *refs):
    pieces, (rows_out, keep, send, stack) = refs[:-4], refs[-4:]
    half = w_gate.shape[1] // 2
    rows = take_rows(0, pieces, stack)
    rows_out[...] = rows
    for target, far in ((send, True), (keep, False)):
        columns = core_columns(half, far)
        target[:, :half] = dot(rows, w_gate[:, columns]).astype(BF16)
        target[:, half:] = dot(rows, w_up[:, columns]).astype(BF16)


def hidden_body(w_down, *refs):
    pieces, (keep, send, stack) = refs[:-3], refs[-3:]
    half = w_down.shape[0] // 2
    rows = take_rows(CAP, pieces, stack)
    for target, far in ((send, True), (keep, False)):
        target[...] = dot(rows, w_down[core_columns(half, far), :], 1, 1).astype(BF16)


def transpose_body(after, rows_ref, out):
    rows = rows_ref[...]
    count = rows.shape[0]
    same = (iota((count, count), 0) == iota((count, count), 1)).astype(F32).astype(BF16)
    out[...] = dot(rows, same, 0, 0).astype(BF16)


def activate_body(after, pre_own, pre_far, hid_own, hid_far, acts):
    half = hid_own.shape[1]
    pre = pre_own[...].astype(F32) + pre_far[...].astype(F32)
    hidden_grad = hid_own[...].astype(F32) + hid_far[...].astype(F32)
    gate_pre = pre[:, :half]
    up_pre = pre[:, half:]
    sigma = jax.nn.sigmoid(gate_pre)
    acts[:, :half] = (hidden_grad * up_pre * sigma * (1.0 + gate_pre * (1.0 - sigma))).astype(BF16)
    acts[:, half:] = (hidden_grad * gate_pre * sigma).astype(BF16)


def fold_rows(rows, fold):
    width = rows.shape[1] // fold
    return [
        jnp.concatenate(
            [rows[place : place + CAP, part * width : (part + 1) * width] for part in range(fold)],
            axis=0,
        )
        for place in range(0, rows.shape[0], CAP)
    ]


def back_part(w_gate, w_up, acts, sibling):
    half = w_gate.shape[1] // 2
    columns = core_columns(half, sibling)
    part = dot(acts[:, :half], w_gate[:, columns], 1, 1)
    return part + dot(acts[:, half:], w_up[:, columns], 1, 1)


def back_own_body(w_gate, w_up, acts, total):
    total[...] = back_part(w_gate, w_up, acts, False)


def back_far_body(w_gate, w_up, acts, own, *outs):
    count = outs[0].shape[0]
    total = own[...] + back_part(w_gate, w_up, acts, True)
    for place, out in enumerate(outs):
        out[...] = total[place * count : (place + 1) * count].astype(BF16)


def weight_body(which, chunks, after, rows_ref, acts_own, acts_far, out, token, tile, sems):
    token[...] = jnp.zeros_like(token)
    half = out.shape[1] // 2
    depth = out.shape[0] // chunks
    columns = slice(which * half, (which + 1) * half)
    stores = []
    for chunk in range(chunks):
        span = slice(chunk * depth, (chunk + 1) * depth)
        rows = rows_ref[span, :]
        for acts, far in ((acts_own, False), (acts_far, True)):
            tile[span, core_columns(half, far)] = dot(rows, acts[:, columns]).astype(BF16)
        stores.append(pltpu.make_async_copy(tile.at[span], out.at[span], sems.at[chunk]))
        stores[-1].start()
    for store in stores:
        store.wait()


def gather_body(fold, experts, after, *refs):
    parts, outs = refs[:HSPLIT], refs[HSPLIT:]
    total = parts[0][...].astype(F32) + parts[1][...].astype(F32)
    total = total + (parts[2][...].astype(F32) + parts[3][...].astype(F32))
    for out, rows in zip(outs, fold_rows(total, fold)):
        out[...] = rows.astype(BF16)


def scatter_body(fold, *refs):
    picks, pieces = refs[:fold], refs[fold:-4]
    out, stack, tile, sems = refs[-4:]
    width = out.shape[1] // fold
    piece = CAP * fold
    for place, ref in enumerate(pieces):
        stack[place * piece : (place + 1) * piece, :] = ref[...].astype(F32)
    returned = stack[...].astype(BF16)
    stores = []
    for part in range(fold):
        for span in column_spans(width):
            target = slice(part * width + span.start, part * width + span.stop)
            tile[:, target] = dot(picks[part][...], returned[:, span], 0, 0).astype(BF16)
            store = pltpu.make_async_copy(
                tile.at[:, target], out.at[:, target], sems.at[len(stores)]
            )
            store.start()
            stores.append(store)
    for store in stores:
        store.wait()


def per_device(out_grad, inputs, expert_ids, gate_weights, w_gate, w_up, w_down):
    devices = lax.axis_size("expert")
    spread = lax.axis_size("dp")
    experts = devices // HSPLIT
    tokens, features = out_grad.shape
    routed = expert_ids.shape[1]
    fold = fold_of(features)
    hidden = w_gate.shape[1]
    half = hidden // 2
    count = devices * CAP
    product = 2 * count * features * hidden
    dma = pltpu.SemaphoreType.DMA

    def to_expert(value, step):
        pairs = [(d, (d + step * HSPLIT) % devices) for d in range(devices)]
        return lax.ppermute(value, "expert", pairs)

    def to_peer(value, flip):
        return lax.ppermute(value, "expert", [(d, d ^ flip) for d in range(devices)])

    def to_dp(value, flip):
        return lax.ppermute(value, "dp", [(d, d ^ flip) for d in range(spread)])

    picked = run(
        functools.partial(pick_body, experts, fold),
        (shape((experts * fold * CAP, tokens)),) * fold
        + (shape((2 * CAP, features)),) * experts,
        [HBM] * 4,
        8 * experts * CAP * tokens * features,
        4 * tokens * features,
        *(in_hbm(array) for array in (expert_ids.T, gate_weights.T, out_grad, inputs)),
        scratch=(
            pltpu.VMEM((routed, tokens), jnp.int32),
            pltpu.VMEM((routed, tokens), F32),
            pltpu.VMEM((tokens, features), BF16),
            pltpu.VMEM((tokens, features), BF16),
            dma((2 + 2 * len(column_spans(features)),)),
        ),
    )
    picks, own = picked[:fold], picked[fold:]
    weights = (w_gate, w_up, w_down)
    gate_here, up_here, down_here = run(
        functools.partial(load_body, 4),
        tuple(pltpu.VMEM(weight.shape, weight.dtype) for weight in weights),
        [ANY] + [HBM] * 3,
        0,
        6 * features * hidden,
        picks[0],
        *(in_hbm(weight) for weight in weights),
        scratch=(dma((12,)),),
    )

    away = [to_expert(own[step], step) for step in range(1, experts)]
    near = [own[0]] + [to_peer(own[0], flip) for flip in range(1, HSPLIT)]
    away = away[0] if len(away) == 1 else jnp.concatenate(away, axis=0)
    far = [away] + [to_peer(away, flip) for flip in range(1, HSPLIT)]
    pieces = [array for pair in zip(near, far) for array in pair]

    stack = pltpu.VMEM((2 * count, features), F32)
    rows_input, pre_keep, pre_send = run(
        forward_body,
        (shape((count, features)), shape((count, hidden)), shape((count, hidden))),
        [VMEM] * (2 + len(pieces)),
        2 * product,
        4 * features * hidden,
        gate_here,
        up_here,
        *pieces,
        scratch=(stack,),
    )

    def spread_sum(keep, send):
        near = (keep.astype(F32) + to_dp(send, 1).astype(F32)).astype(BF16)
        flip = 2
        far = jnp.zeros_like(near)
        while flip < spread:
            far = to_dp(near, flip)
            flip *= 2
            if flip < spread:
                near = (near.astype(F32) + far.astype(F32)).astype(BF16)
        return near, far

    pre_own, pre_far = spread_sum(pre_keep, pre_send)
    hid_keep, hid_send = run(
        hidden_body,
        (shape((count, half)), shape((count, half))),
        [VMEM] * (1 + len(pieces)),
        product,
        2 * features * hidden,
        down_here,
        *pieces,
        scratch=(stack,),
    )
    hid_own, hid_far = spread_sum(hid_keep, hid_send)
    rows_across = run(
        transpose_body,
        shape((features, count)),
        [ANY, VMEM],
        0,
        0,
        hid_own,
        rows_input,
    )
    acts = run(
        activate_body,
        shape((count, hidden)),
        [ANY] + [VMEM] * 4,
        20 * count * half,
        10 * count * half,
        rows_across,
        pre_own,
        pre_far,
        hid_own,
        hid_far,
    )
    acts_far = to_dp(acts, 1)
    back_own = run(
        back_own_body,
        shape((count, features), F32),
        [VMEM] * 3,
        product,
        2 * features * hidden,
        gate_here,
        up_here,
        acts,
    )
    back = run(
        back_far_body,
        (shape((count // HSPLIT, features)),) * HSPLIT,
        [VMEM] * 4,
        product,
        2 * features * hidden,
        gate_here,
        up_here,
        acts_far,
        back_own,
    )

    def weight_grad(which, after):
        chunks = features // 256 if features % 256 == 0 else 2
        return run(
            functools.partial(weight_body, which, chunks),
            (shape((features, hidden)), shape((8, 128), F32)),
            [ANY] + [VMEM] * 3,
            0,
            0,
            after,
            rows_across,
            acts,
            acts_far,
            out_spec=(HBM, VMEM),
            scratch=(pltpu.VMEM((features, hidden), BF16), dma((chunks,))),
        )

    grad_gate, token = weight_grad(0, back[0])
    summed = run(
        functools.partial(gather_body, fold, experts),
        (shape((CAP * fold, features // fold)),) * experts,
        [ANY] + [VMEM] * HSPLIT,
        0,
        0,
        token,
        *(to_peer(back[flip], flip) for flip in range(HSPLIT - 1, 0, -1)),
        back[0],
    )
    grad_up, _ = weight_grad(1, summed[0])
    returned = [summed[0]] + [to_expert(summed[step], experts - step) for step in range(1, experts)]
    in_grad = run(
        functools.partial(scatter_body, fold),
        shape((tokens, features)),
        [VMEM] * (fold + experts),
        4 * experts * CAP * tokens * features,
        2 * tokens * features,
        *picks,
        *returned,
        out_spec=HBM,
        scratch=(
            pltpu.VMEM((experts * fold * CAP, features // fold), F32),
            pltpu.VMEM((tokens, features), BF16),
            dma((fold * len(column_spans(features // fold)),)),
        ),
    )
    return (in_grad, grad_gate, grad_up)


def solution(mesh):
    placed = (
        P("expert", "dp"),
        P("expert", "dp"),
        P("expert", None),
        P("expert", None),
        P("dp", "expert"),
        P("dp", "expert"),
        P("expert", "dp"),
    )
    return jax.shard_map(
        per_device,
        mesh=mesh,
        in_specs=placed,
        out_specs=(P("expert", "dp"), P("dp", "expert"), P("dp", "expert")),
        check_vma=False,
    )
```

```python
import functools

import jax
import jax.numpy as jnp
from jax import lax
from jax.experimental import pallas as pl
from jax.experimental.pallas import tpu as pltpu
from jax.sharding import PartitionSpec as P

HSPLIT = 4
CAP = 12
F32 = jnp.float32
BF16 = jnp.bfloat16
VMEM = pl.BlockSpec(memory_space=pltpu.VMEM)
HBM = pl.BlockSpec(memory_space=pltpu.HBM)
ANY = pl.BlockSpec(memory_space=pl.ANY)


def shape(dims, dtype=BF16):
    return jax.ShapeDtypeStruct(dims, dtype)


def run(body, outs, specs, flops, nbytes, *args, out_spec=VMEM, scratch=()):
    return pl.pallas_call(
        body,
        out_shape=outs,
        in_specs=specs,
        out_specs=out_spec if isinstance(out_spec, tuple) else jax.tree.map(lambda _: out_spec, outs),
        scratch_shapes=scratch,
        compiler_params=pltpu.CompilerParams(vmem_limit_bytes=40 * 1024 * 1024),
        cost_estimate=pl.CostEstimate(flops=flops, bytes_accessed=nbytes, transcendentals=0),
    )(*args)


def in_hbm(value):
    return pltpu.with_memory_space_constraint(value, pltpu.HBM)


def dot(left, right, left_dim=1, right_dim=0):
    return lax.dot_general(
        left, right, (((left_dim,), (right_dim,)), ((), ())), preferred_element_type=F32
    )


def iota(dims, dim):
    return lax.broadcasted_iota(jnp.int32, dims, dim)


def over_cap(rows):
    return jnp.floor((rows.astype(F32) + 0.5) * (1.0 / CAP)).astype(jnp.int32)


def column_spans(width):
    whole = width // 128 * 128
    if whole != width or width < 512:
        return [slice(0, width)]
    middle = width // 256 * 128
    return [slice(0, middle), slice(middle, width)]


def core_columns(width, far):
    side = lax.rem(lax.axis_index("dp"), 2)
    side = 1 - side if far else side
    return pl.ds(pl.multiple_of(side * width, width), width)


def fold_of(width):
    return 2 if width % 256 == 0 else 1


def pick_body(experts, fold, ids_hbm, gates_hbm, grads_hbm, inputs_hbm, *refs):
    picks, pieces = refs[:fold], refs[fold : fold + experts]
    ids, gates, grads, inputs, sems = refs[fold + experts :]
    spans = column_spans(grads.shape[1])
    moves = [(ids_hbm, ids), (gates_hbm, gates)]
    for span in spans:
        moves.append((inputs_hbm.at[:, span], inputs.at[:, span]))
        moves.append((grads_hbm.at[:, span], grads.at[:, span]))
    loads = [
        pltpu.make_async_copy(source, target, sems.at[place])
        for place, (source, target) in enumerate(moves)
    ]
    for load in loads:
        load.start()
    tokens = ids.shape[1]
    padded = max(8, experts)
    group = lax.div(lax.axis_index("expert"), HSPLIT)
    earlier = (iota((tokens, tokens), 0) < iota((tokens, tokens), 1)).astype(F32).astype(BF16)
    loads[0].wait()
    loads[1].wait()
    expert_ids = ids[...]
    route_gates = gates[...]
    match_rows = jnp.zeros((padded, tokens), F32)
    matches = []
    token_gates = []
    for step in range(experts):
        hits = expert_ids == lax.rem(group + step, experts)
        match = jnp.sum(hits.astype(F32), axis=0, keepdims=True)
        matches.append(match)
        token_gates.append(jnp.sum(jnp.where(hits, route_gates, 0.0), axis=0, keepdims=True))
        match_rows = jnp.where(iota((padded, tokens), 0) == step, match, match_rows)
    counts = dot(match_rows.astype(BF16), earlier)
    slots = [
        jnp.where(matches[step] > 0.0, counts[step : step + 1, :], -1.0e6)
        for step in range(experts)
    ]

    def chosen(rows, offset):
        places = (iota((rows, tokens), 0) - offset).astype(F32)
        return [(places == slots[step]).astype(F32) for step in range(experts)]

    input_picks = chosen(2 * CAP, 0)
    grad_picks = chosen(2 * CAP, CAP)
    slot_gates = [
        jnp.sum(hit * gate, axis=1, keepdims=True) for hit, gate in zip(grad_picks, token_gates)
    ]
    gate_column = jnp.concatenate(slot_gates, axis=0)
    input_picks = jnp.concatenate(input_picks, axis=0)
    grad_picks = jnp.concatenate(grad_picks, axis=0)
    if fold == 2:
        picks[0][...] = input_picks.astype(BF16)
        picks[1][...] = grad_picks.astype(BF16)
    else:
        picks[0][...] = jnp.concatenate(chosen(CAP, 0), axis=0).astype(BF16)
    input_picks = input_picks.astype(BF16)
    grad_picks = grad_picks.astype(BF16)
    for place, span in enumerate(spans):
        loads[2 + 2 * place].wait()
        total = dot(input_picks, inputs[:, span])
        loads[3 + 2 * place].wait()
        total = total + dot(grad_picks, grads[:, span]) * gate_column
        for step in range(experts):
            rows = slice(step * 2 * CAP, (step + 1) * 2 * CAP)
            pieces[step][:, span] = total[rows].astype(BF16)


def load_body(parts, after, *refs):
    count = len(refs) // 2 - 1
    token, sems = refs[-2:]
    token[...] = jnp.zeros_like(token)
    loads = []
    for place in range(count):
        depth = refs[place].shape[0] // parts
        for part in range(parts):
            rows = slice(part * depth, (part + 1) * depth)
            source, target = refs[place].at[rows], refs[count + place].at[rows]
            loads.append(pltpu.make_async_copy(source, target, sems.at[len(loads)]))
    for load in loads:
        load.start()
    for load in loads:
        load.wait()


def take_rows(pieces, stack):
    place = 0
    for ref in pieces:
        stack[place : place + ref.shape[0], :] = ref[...].astype(F32)
        place += ref.shape[0]
    stacked = stack[...].astype(BF16)
    count = place // 2
    rows = iota((count, place), 0)
    source = rows + over_cap(rows) * CAP
    taken = []
    for offset in (0, CAP):
        mover = (iota((count, place), 1) == source + offset).astype(F32).astype(BF16)
        taken.append(dot(mover, stacked).astype(BF16))
    return taken


def pre_part(rows, weight, place, keep, send):
    half = weight.shape[1] // 2
    span = slice(place * half, (place + 1) * half)
    for target, far in ((send, True), (keep, False)):
        target[:, span] = dot(rows, weight[:, core_columns(half, far)]).astype(BF16)


def hidden_part(rows, weight, keep, send):
    half = weight.shape[0] // 2
    for target, far in ((send, True), (keep, False)):
        part = dot(rows, weight[core_columns(half, far), :], 1, 1)
        target[:, 2 * half :] = part.astype(BF16)


def rows_body(after, w_gate, w_up, w_down, *refs):
    pieces = refs[:-4][::-1]
    rows_out, keep, send, stack = refs[-4:]
    input_rows, grad_rows = take_rows(pieces, stack)
    rows_out[...] = input_rows
    pre_part(input_rows, w_gate, 0, keep, send)
    pre_part(input_rows, w_up, 1, keep, send)
    hidden_part(grad_rows, w_down, keep, send)


def transpose_body(after, near, far, out):
    rows = jnp.concatenate([near[...], far[...]], axis=0)
    count = rows.shape[0]
    same = (iota((count, count), 0) == iota((count, count), 1)).astype(F32).astype(BF16)
    out[...] = dot(rows, same, 0, 0).astype(BF16)


def core_sum_body(own, other, *refs):
    refs[-1][...] = (own[...].astype(F32) + other[...].astype(F32)).astype(BF16)


def activate_body(own, other, *refs):
    acts = refs[-1]
    half = own.shape[1] // 3
    total = own[...].astype(F32) + other[...].astype(F32)
    gate_pre = total[:, :half]
    up_pre = total[:, half : 2 * half]
    hidden_grad = total[:, 2 * half :]
    sigma = jax.nn.sigmoid(gate_pre)
    acts[:, :half] = (hidden_grad * up_pre * sigma * (1.0 + gate_pre * (1.0 - sigma))).astype(BF16)
    acts[:, half:] = (hidden_grad * gate_pre * sigma).astype(BF16)


def fold_rows(rows, fold):
    width = rows.shape[1] // fold
    return [
        jnp.concatenate(
            [rows[place : place + CAP, part * width : (part + 1) * width] for part in range(fold)],
            axis=0,
        )
        for place in range(0, rows.shape[0], CAP)
    ]


def back_part(experts, w_gate, w_up, near, far, sibling):
    half = w_gate.shape[1] // 2
    acts = jnp.concatenate([near[...], far[...]], axis=0)
    count = acts.shape[0]
    rows = iota((count, count), 0)
    group = CAP * experts
    peer = jnp.floor((rows.astype(F32) + 0.5) * (1.0 / group)).astype(jnp.int32)
    inner = rows - peer * group
    source = jnp.where(
        inner < CAP,
        peer * CAP + inner,
        HSPLIT * CAP + peer * (group - CAP) + inner - CAP,
    )
    mover = (iota((count, count), 1) == source).astype(F32).astype(BF16)
    acts = dot(mover, acts).astype(BF16)
    columns = core_columns(half, sibling)
    part = dot(acts[:, :half], w_gate[:, columns], 1, 1)
    return part + dot(acts[:, half:], w_up[:, columns], 1, 1)


def back_own_body(experts, w_gate, w_up, near, far, total):
    total[...] = back_part(experts, w_gate, w_up, near, far, False)


def back_far_body(experts, w_gate, w_up, near, far, own, *outs):
    count = outs[0].shape[0]
    total = own[...] + back_part(experts, w_gate, w_up, near, far, True)
    for place, out in enumerate(outs):
        out[...] = total[place * count : (place + 1) * count].astype(BF16)


def weight_body(
    which, chunks, after, rows_ref, own_near, own_far, sib_near, sib_far, out, token, tile, sems
):
    token[...] = jnp.zeros_like(token)
    half = out.shape[1] // 2
    depth = out.shape[0] // chunks
    columns = slice(which * half, (which + 1) * half)
    own = jnp.concatenate([own_near[:, columns], own_far[:, columns]], axis=0)
    sib = jnp.concatenate([sib_near[:, columns], sib_far[:, columns]], axis=0)
    stores = []
    for chunk in range(chunks):
        span = slice(chunk * depth, (chunk + 1) * depth)
        rows = rows_ref[span, :]
        for acts, far in ((own, False), (sib, True)):
            tile[span, core_columns(half, far)] = dot(rows, acts).astype(BF16)
        stores.append(pltpu.make_async_copy(tile.at[span], out.at[span], sems.at[chunk]))
        stores[-1].start()
    for store in stores:
        store.wait()


def gather_body(fold, experts, after, *refs):
    parts, outs = refs[:HSPLIT], refs[HSPLIT:]
    total = parts[0][...].astype(F32) + parts[1][...].astype(F32)
    total = total + (parts[2][...].astype(F32) + parts[3][...].astype(F32))
    for out, rows in zip(outs, fold_rows(total, fold)):
        out[...] = rows.astype(BF16)


def scatter_body(fold, *refs):
    picks, pieces = refs[:fold], refs[fold:-4]
    out, stack, tile, sems = refs[-4:]
    width = out.shape[1] // fold
    piece = CAP * fold
    for place, ref in enumerate(pieces):
        stack[place * piece : (place + 1) * piece, :] = ref[...].astype(F32)
    returned = stack[...].astype(BF16)
    stores = []
    for part in range(fold):
        for span in column_spans(width):
            target = slice(part * width + span.start, part * width + span.stop)
            tile[:, target] = dot(picks[part][...], returned[:, span], 0, 0).astype(BF16)
            store = pltpu.make_async_copy(
                tile.at[:, target], out.at[:, target], sems.at[len(stores)]
            )
            store.start()
            stores.append(store)
    for store in stores:
        store.wait()


def per_device(out_grad, inputs, expert_ids, gate_weights, w_gate, w_up, w_down):
    devices = lax.axis_size("expert")
    spread = lax.axis_size("dp")
    experts = devices // HSPLIT
    tokens, features = out_grad.shape
    routed = expert_ids.shape[1]
    fold = fold_of(features)
    hidden = w_gate.shape[1]
    half = hidden // 2
    count = devices * CAP
    product = 2 * count * features * hidden
    dma = pltpu.SemaphoreType.DMA

    def to_expert(value, step):
        pairs = [(d, (d + step * HSPLIT) % devices) for d in range(devices)]
        return lax.ppermute(value, "expert", pairs)

    def to_peer(value, flip):
        return lax.ppermute(value, "expert", [(d, d ^ flip) for d in range(devices)])

    def to_dp(value, flip):
        return lax.ppermute(value, "dp", [(d, d ^ flip) for d in range(spread)])

    picked = run(
        functools.partial(pick_body, experts, fold),
        (shape((experts * fold * CAP, tokens)),) * fold
        + (shape((2 * CAP, features)),) * experts,
        [HBM] * 4,
        8 * experts * CAP * tokens * features,
        4 * tokens * features,
        *(in_hbm(array) for array in (expert_ids.T, gate_weights.T, out_grad, inputs)),
        scratch=(
            pltpu.VMEM((routed, tokens), jnp.int32),
            pltpu.VMEM((routed, tokens), F32),
            pltpu.VMEM((tokens, features), BF16),
            pltpu.VMEM((tokens, features), BF16),
            dma((2 + 2 * len(column_spans(features)),)),
        ),
    )
    picks, own = picked[:fold], picked[fold:]
    weights = (w_up, w_down)
    up_here, down_here, loaded = run(
        functools.partial(load_body, 4),
        tuple(pltpu.VMEM(weight.shape, weight.dtype) for weight in weights)
        + (shape((8, 128), F32),),
        [ANY] + [HBM] * 2,
        0,
        4 * features * hidden,
        picks[0],
        *(in_hbm(weight) for weight in weights),
        scratch=(dma((8,)),),
    )

    away = [to_expert(own[step], step) for step in range(1, experts)]
    near = [own[0]] + [to_peer(own[0], flip) for flip in range(1, HSPLIT)]
    away = away[0] if len(away) == 1 else jnp.concatenate(away, axis=0)
    away, loaded = lax.optimization_barrier((away, loaded))
    far = [away] + [to_peer(away, flip) for flip in range(1, HSPLIT)]

    def multiply(after, pieces, flops):
        rows = sum(piece.shape[0] for piece in pieces) // 2
        return run(
            rows_body,
            (shape((rows, features)), shape((rows, 3 * half)), shape((rows, 3 * half))),
            [ANY] + [VMEM] * (3 + len(pieces)),
            flops,
            0,
            after,
            w_gate,
            up_here,
            down_here,
            *pieces[::-1],
            scratch=(pltpu.VMEM((2 * rows, features), F32),),
        )

    def core_sum(keep, send, after):
        return run(
            core_sum_body,
            shape(keep.shape),
            [VMEM] * 2 + [ANY],
            0,
            0,
            keep,
            to_dp(send, 1),
            after,
        )

    def activate(total, after):
        flip = 2
        other = jnp.zeros_like(total)
        while flip < spread:
            other = to_dp(total, flip)
            flip *= 2
            if flip < spread:
                total = (total.astype(F32) + other.astype(F32)).astype(BF16)
        rows = total.shape[0]
        return run(
            activate_body,
            shape((rows, hidden)),
            [VMEM] * 2 + [ANY],
            20 * rows * half,
            10 * rows * half,
            total,
            other,
            after,
        )

    rows_near, near_keep, near_send = multiply(away, near, 3 * product)
    near_sum = core_sum(near_keep, near_send, away)
    rows_far, far_keep, far_send = multiply(near_sum, far, 0)
    acts_near = activate(near_sum, away)
    far_sum = core_sum(far_keep, far_send, acts_near)
    rows_across = run(
        transpose_body,
        shape((features, count)),
        [ANY] + [VMEM] * 2,
        0,
        0,
        far_sum,
        rows_near,
        rows_far,
    )
    acts_far = activate(far_sum, rows_across)
    sib_near = to_dp(acts_near, 1)
    sib_far = to_dp(acts_far, 1)
    back_own = run(
        functools.partial(back_own_body, experts),
        shape((count, features), F32),
        [VMEM] * 4,
        product,
        2 * features * hidden,
        w_gate,
        up_here,
        acts_near,
        acts_far,
    )
    back = run(
        functools.partial(back_far_body, experts),
        (shape((count // HSPLIT, features)),) * HSPLIT,
        [VMEM] * 5,
        product,
        2 * features * hidden,
        w_gate,
        up_here,
        sib_near,
        sib_far,
        back_own,
    )

    def weight_grad(which, after):
        chunks = features // 256 if features % 256 == 0 else 2
        return run(
            functools.partial(weight_body, which, chunks),
            (shape((features, hidden)), shape((8, 128), F32)),
            [ANY] + [VMEM] * 5,
            0,
            0,
            after,
            rows_across,
            acts_near,
            acts_far,
            sib_near,
            sib_far,
            out_spec=(HBM, VMEM),
            scratch=(pltpu.VMEM((features, hidden), BF16), dma((chunks,))),
        )

    grad_gate, token = weight_grad(0, back[0])
    summed = run(
        functools.partial(gather_body, fold, experts),
        (shape((CAP * fold, features // fold)),) * experts,
        [ANY] + [VMEM] * HSPLIT,
        0,
        0,
        token,
        *(to_peer(back[flip], flip) for flip in range(HSPLIT - 1, 0, -1)),
        back[0],
    )
    grad_up, _ = weight_grad(1, summed[0])
    returned = [summed[0]] + [to_expert(summed[step], experts - step) for step in range(1, experts)]
    in_grad = run(
        functools.partial(scatter_body, fold),
        shape((tokens, features)),
        [VMEM] * (fold + experts),
        4 * experts * CAP * tokens * features,
        2 * tokens * features,
        *picks,
        *returned,
        out_spec=HBM,
        scratch=(
            pltpu.VMEM((experts * fold * CAP, features // fold), F32),
            pltpu.VMEM((tokens, features), BF16),
            dma((fold * len(column_spans(features // fold)),)),
        ),
    )
    return (in_grad, grad_gate, grad_up)


def solution(mesh):
    placed = (
        P("expert", "dp"),
        P("expert", "dp"),
        P("expert", None),
        P("expert", None),
        P("dp", "expert"),
        P("dp", "expert"),
        P("expert", "dp"),
    )
    return jax.shard_map(
        per_device,
        mesh=mesh,
        in_specs=placed,
        out_specs=(P("expert", "dp"), P("dp", "expert"), P("dp", "expert")),
        check_vma=False,
    )
```

```python
import functools

import jax
import jax.numpy as jnp
from jax import lax
from jax.experimental import pallas as pl
from jax.experimental.pallas import tpu as pltpu
from jax.sharding import PartitionSpec as P

HSPLIT = 4
CAP = 12
F32 = jnp.float32
BF16 = jnp.bfloat16
VMEM = pl.BlockSpec(memory_space=pltpu.VMEM)
HBM = pl.BlockSpec(memory_space=pltpu.HBM)
ANY = pl.BlockSpec(memory_space=pl.ANY)


def shape(dims, dtype=BF16):
    return jax.ShapeDtypeStruct(dims, dtype)


def run(body, outs, specs, flops, nbytes, *args, out_spec=VMEM, scratch=()):
    return pl.pallas_call(
        body,
        out_shape=outs,
        in_specs=specs,
        out_specs=out_spec if isinstance(out_spec, tuple) else jax.tree.map(lambda _: out_spec, outs),
        scratch_shapes=scratch,
        compiler_params=pltpu.CompilerParams(vmem_limit_bytes=40 * 1024 * 1024),
        cost_estimate=pl.CostEstimate(flops=flops, bytes_accessed=nbytes, transcendentals=0),
    )(*args)


def in_hbm(value):
    return pltpu.with_memory_space_constraint(value, pltpu.HBM)


def dot(left, right, left_dim=1, right_dim=0):
    return lax.dot_general(
        left, right, (((left_dim,), (right_dim,)), ((), ())), preferred_element_type=F32
    )


def iota(dims, dim):
    return lax.broadcasted_iota(jnp.int32, dims, dim)


def over_cap(rows):
    return jnp.floor((rows.astype(F32) + 0.5) * (1.0 / CAP)).astype(jnp.int32)


def column_spans(width):
    whole = width // 128 * 128
    if whole != width or width < 512:
        return [slice(0, width)]
    middle = width // 256 * 128
    return [slice(0, middle), slice(middle, width)]


def core_columns(width, far):
    side = lax.rem(lax.axis_index("dp"), 2)
    side = 1 - side if far else side
    return pl.ds(pl.multiple_of(side * width, width), width)


def fold_of(width):
    return 2 if width % 256 == 0 else 1


def pick_body(experts, fold, ids_hbm, gates_hbm, grads_hbm, inputs_hbm, *refs):
    picks, pieces = refs[:fold], refs[fold : fold + experts]
    ids, gates, grads, inputs, sems = refs[fold + experts :]
    spans = column_spans(grads.shape[1])
    moves = [(ids_hbm, ids), (gates_hbm, gates)]
    for span in spans:
        moves.append((inputs_hbm.at[:, span], inputs.at[:, span]))
        moves.append((grads_hbm.at[:, span], grads.at[:, span]))
    loads = [
        pltpu.make_async_copy(source, target, sems.at[place])
        for place, (source, target) in enumerate(moves)
    ]
    for load in loads:
        load.start()
    tokens = ids.shape[1]
    padded = max(8, experts)
    group = lax.div(lax.axis_index("expert"), HSPLIT)
    earlier = (iota((tokens, tokens), 0) < iota((tokens, tokens), 1)).astype(F32).astype(BF16)
    loads[0].wait()
    loads[1].wait()
    expert_ids = ids[...]
    route_gates = gates[...]
    match_rows = jnp.zeros((padded, tokens), F32)
    matches = []
    token_gates = []
    for step in range(experts):
        hits = expert_ids == lax.rem(group + step, experts)
        match = jnp.sum(hits.astype(F32), axis=0, keepdims=True)
        matches.append(match)
        token_gates.append(jnp.sum(jnp.where(hits, route_gates, 0.0), axis=0, keepdims=True))
        match_rows = jnp.where(iota((padded, tokens), 0) == step, match, match_rows)
    counts = dot(match_rows.astype(BF16), earlier)
    slots = [
        jnp.where(matches[step] > 0.0, counts[step : step + 1, :], -1.0e6)
        for step in range(experts)
    ]

    def chosen(rows, offset):
        places = (iota((rows, tokens), 0) - offset).astype(F32)
        return [(places == slots[step]).astype(F32) for step in range(experts)]

    input_picks = chosen(2 * CAP, 0)
    grad_picks = chosen(2 * CAP, CAP)
    slot_gates = [
        jnp.sum(hit * gate, axis=1, keepdims=True) for hit, gate in zip(grad_picks, token_gates)
    ]
    gate_column = jnp.concatenate(slot_gates, axis=0)
    input_picks = jnp.concatenate(input_picks, axis=0)
    grad_picks = jnp.concatenate(grad_picks, axis=0)
    if fold == 2:
        picks[0][...] = input_picks.astype(BF16)
        picks[1][...] = grad_picks.astype(BF16)
    else:
        picks[0][...] = jnp.concatenate(chosen(CAP, 0), axis=0).astype(BF16)
    input_picks = input_picks.astype(BF16)
    grad_picks = grad_picks.astype(BF16)
    for place, span in enumerate(spans):
        loads[2 + 2 * place].wait()
        total = dot(input_picks, inputs[:, span])
        loads[3 + 2 * place].wait()
        total = total + dot(grad_picks, grads[:, span]) * gate_column
        for step in range(experts):
            rows = slice(step * 2 * CAP, (step + 1) * 2 * CAP)
            pieces[step][:, span] = total[rows].astype(BF16)


def load_body(parts, after, *refs):
    hbm, (w_gate, w_up, down_across, w_down, sems) = refs[:3], refs[3:]
    loads = []
    for source, target in zip((hbm[2], hbm[0], hbm[1]), (w_down, w_gate, w_up)):
        depth = source.shape[0] // parts
        for part in range(parts):
            rows = slice(part * depth, (part + 1) * depth)
            loads.append(
                pltpu.make_async_copy(source.at[rows], target.at[rows], sems.at[len(loads)])
            )
    for load in loads:
        load.start()
    for load in loads[:parts]:
        load.wait()
    down_across[...] = w_down[...].T
    for load in loads[parts:]:
        load.wait()


def take_rows(offset, pieces):
    rows = []
    for ref in pieces[::-1]:
        piece = ref[...].astype(F32)
        for place in range(offset, piece.shape[0], 2 * CAP):
            rows.append(piece[place : place + CAP])
    return jnp.concatenate(rows, axis=0).astype(BF16)


def forward_body(w_gate, w_up, *refs):
    pieces, (rows_out, keep, send) = refs[:-3], refs[-3:]
    half = w_gate.shape[1] // 2
    rows = take_rows(0, pieces)
    rows_out[...] = rows
    for target, far in ((send, True), (keep, False)):
        columns = core_columns(half, far)
        target[:, :half] = dot(rows, w_gate[:, columns]).astype(BF16)
        target[:, half:] = dot(rows, w_up[:, columns]).astype(BF16)


def hidden_body(down_across, *refs):
    pieces, (keep, send) = refs[:-2], refs[-2:]
    half = down_across.shape[1] // 2
    rows = take_rows(CAP, pieces)
    for target, far in ((send, True), (keep, False)):
        target[...] = dot(rows, down_across[:, core_columns(half, far)]).astype(BF16)


def transpose_body(after, rows_ref, w_gate, w_up, rows_across, gate_across, up_across):
    rows = rows_ref[...]
    count = rows.shape[0]
    same = (iota((count, count), 0) == iota((count, count), 1)).astype(F32).astype(BF16)
    rows_across[...] = dot(rows, same, 0, 0).astype(BF16)
    gate_across[...] = w_gate[...].T
    up_across[...] = w_up[...].T


def activate_body(after, pre_own, pre_far, hid_own, hid_far, acts):
    half = hid_own.shape[1]
    pre = pre_own[...].astype(F32) + pre_far[...].astype(F32)
    hidden_grad = hid_own[...].astype(F32) + hid_far[...].astype(F32)
    gate_pre = pre[:, :half]
    up_pre = pre[:, half:]
    sigma = jax.nn.sigmoid(gate_pre)
    acts[:, :half] = (hidden_grad * up_pre * sigma * (1.0 + gate_pre * (1.0 - sigma))).astype(BF16)
    acts[:, half:] = (hidden_grad * gate_pre * sigma).astype(BF16)


def fold_rows(rows, fold):
    width = rows.shape[1] // fold
    return [
        jnp.concatenate(
            [rows[place : place + CAP, part * width : (part + 1) * width] for part in range(fold)],
            axis=0,
        )
        for place in range(0, rows.shape[0], CAP)
    ]


def back_part(gate_across, up_across, acts, sibling):
    half = gate_across.shape[0] // 2
    units = core_columns(half, sibling)
    part = dot(acts[:, :half], gate_across[units, :])
    return part + dot(acts[:, half:], up_across[units, :])


def back_own_body(gate_across, up_across, acts, total):
    total[...] = back_part(gate_across, up_across, acts, False)


def back_far_body(gate_across, up_across, acts, own, *outs):
    count = outs[0].shape[0]
    total = own[...] + back_part(gate_across, up_across, acts, True)
    for place, out in enumerate(outs):
        out[...] = total[place * count : (place + 1) * count].astype(BF16)


def weight_body(which, chunks, after, rows_ref, acts_own, acts_far, out, token, tile, sems):
    token[...] = jnp.zeros_like(token)
    half = out.shape[1] // 2
    depth = out.shape[0] // chunks
    columns = slice(which * half, (which + 1) * half)
    stores = []
    for chunk in range(chunks):
        span = slice(chunk * depth, (chunk + 1) * depth)
        rows = rows_ref[span, :]
        for acts, far in ((acts_own, False), (acts_far, True)):
            tile[span, core_columns(half, far)] = dot(rows, acts[:, columns]).astype(BF16)
        stores.append(pltpu.make_async_copy(tile.at[span], out.at[span], sems.at[chunk]))
        stores[-1].start()
    for store in stores:
        store.wait()


def gather_body(fold, experts, after, *refs):
    parts, outs = refs[:HSPLIT], refs[HSPLIT:]
    total = parts[0][...].astype(F32) + parts[1][...].astype(F32)
    total = total + (parts[2][...].astype(F32) + parts[3][...].astype(F32))
    for out, rows in zip(outs, fold_rows(total, fold)):
        out[...] = rows.astype(BF16)


def scatter_body(fold, *refs):
    picks, pieces = refs[:fold], refs[fold:-4]
    out, stack, tile, sems = refs[-4:]
    width = out.shape[1] // fold
    piece = CAP * fold
    for place, ref in enumerate(pieces):
        stack[place * piece : (place + 1) * piece, :] = ref[...].astype(F32)
    returned = stack[...].astype(BF16)
    stores = []
    for part in range(fold):
        for span in column_spans(width):
            target = slice(part * width + span.start, part * width + span.stop)
            tile[:, target] = dot(picks[part][...], returned[:, span], 0, 0).astype(BF16)
            store = pltpu.make_async_copy(
                tile.at[:, target], out.at[:, target], sems.at[len(stores)]
            )
            store.start()
            stores.append(store)
    for store in stores:
        store.wait()


def per_device(out_grad, inputs, expert_ids, gate_weights, w_gate, w_up, w_down):
    devices = lax.axis_size("expert")
    spread = lax.axis_size("dp")
    experts = devices // HSPLIT
    tokens, features = out_grad.shape
    routed = expert_ids.shape[1]
    fold = fold_of(features)
    hidden = w_gate.shape[1]
    half = hidden // 2
    count = devices * CAP
    product = 2 * count * features * hidden
    dma = pltpu.SemaphoreType.DMA

    def to_expert(value, step):
        pairs = [(d, (d + step * HSPLIT) % devices) for d in range(devices)]
        return lax.ppermute(value, "expert", pairs)

    def to_peer(value, flip):
        return lax.ppermute(value, "expert", [(d, d ^ flip) for d in range(devices)])

    def to_dp(value, flip):
        return lax.ppermute(value, "dp", [(d, d ^ flip) for d in range(spread)])

    picked = run(
        functools.partial(pick_body, experts, fold),
        (shape((experts * fold * CAP, tokens)),) * fold
        + (shape((2 * CAP, features)),) * experts,
        [HBM] * 4,
        8 * experts * CAP * tokens * features,
        4 * tokens * features,
        *(in_hbm(array) for array in (expert_ids.T, gate_weights.T, out_grad, inputs)),
        scratch=(
            pltpu.VMEM((routed, tokens), jnp.int32),
            pltpu.VMEM((routed, tokens), F32),
            pltpu.VMEM((tokens, features), BF16),
            pltpu.VMEM((tokens, features), BF16),
            dma((2 + 2 * len(column_spans(features)),)),
        ),
    )
    picks, own = picked[:fold], picked[fold:]
    gate_here, up_here, down_across = run(
        functools.partial(load_body, 4),
        tuple(pltpu.VMEM(dims, BF16) for dims in (w_gate.shape, w_up.shape, w_down.shape[::-1])),
        [ANY] + [HBM] * 3,
        0,
        6 * features * hidden,
        picks[0],
        *(in_hbm(weight) for weight in (w_gate, w_up, w_down)),
        scratch=(pltpu.VMEM(w_down.shape, BF16), dma((12,))),
    )

    away = [to_expert(own[step], step) for step in range(1, experts)]
    near = [own[0]] + [to_peer(own[0], flip) for flip in range(1, HSPLIT)]
    away = away[0] if len(away) == 1 else jnp.concatenate(away, axis=0)
    far = [away] + [to_peer(away, flip) for flip in range(1, HSPLIT)]
    pieces = [array for pair in zip(near, far) for array in pair][::-1]

    rows_input, pre_keep, pre_send = run(
        forward_body,
        (shape((count, features)), shape((count, hidden)), shape((count, hidden))),
        [VMEM] * (2 + len(pieces)),
        2 * product,
        4 * features * hidden,
        gate_here,
        up_here,
        *pieces,
    )

    def spread_sum(keep, send):
        near = (keep.astype(F32) + to_dp(send, 1).astype(F32)).astype(BF16)
        flip = 2
        far = jnp.zeros_like(near)
        while flip < spread:
            far = to_dp(near, flip)
            flip *= 2
            if flip < spread:
                near = (near.astype(F32) + far.astype(F32)).astype(BF16)
        return near, far

    pre_own, pre_far = spread_sum(pre_keep, pre_send)
    hid_keep, hid_send = run(
        hidden_body,
        (shape((count, half)), shape((count, half))),
        [VMEM] * (1 + len(pieces)),
        product,
        2 * features * hidden,
        down_across,
        *pieces,
    )
    hid_own, hid_far = spread_sum(hid_keep, hid_send)
    rows_across, gate_across, up_across = run(
        transpose_body,
        (shape((features, count)),) + (shape((hidden, features)),) * 2,
        [ANY] + [VMEM] * 3,
        0,
        0,
        hid_own,
        rows_input,
        gate_here,
        up_here,
    )
    acts = run(
        activate_body,
        shape((count, hidden)),
        [ANY] + [VMEM] * 4,
        20 * count * half,
        10 * count * half,
        rows_across,
        pre_own,
        pre_far,
        hid_own,
        hid_far,
    )
    acts_far = to_dp(acts, 1)
    back_own = run(
        back_own_body,
        shape((count, features), F32),
        [VMEM] * 3,
        product,
        2 * features * hidden,
        gate_across,
        up_across,
        acts,
    )
    back = run(
        back_far_body,
        (shape((count // HSPLIT, features)),) * HSPLIT,
        [VMEM] * 4,
        product,
        2 * features * hidden,
        gate_across,
        up_across,
        acts_far,
        back_own,
    )

    def weight_grad(which, after):
        chunks = features // 256 if features % 256 == 0 else 2
        return run(
            functools.partial(weight_body, which, chunks),
            (shape((features, hidden)), shape((8, 128), F32)),
            [ANY] + [VMEM] * 3,
            0,
            0,
            after,
            rows_across,
            acts,
            acts_far,
            out_spec=(HBM, VMEM),
            scratch=(pltpu.VMEM((features, hidden), BF16), dma((chunks,))),
        )

    grad_gate, token = weight_grad(0, back[0])
    summed = run(
        functools.partial(gather_body, fold, experts),
        (shape((CAP * fold, features // fold)),) * experts,
        [ANY] + [VMEM] * HSPLIT,
        0,
        0,
        token,
        *(to_peer(back[flip], flip) for flip in range(HSPLIT - 1, 0, -1)),
        back[0],
    )
    grad_up, _ = weight_grad(1, summed[0])
    returned = [summed[0]] + [to_expert(summed[step], experts - step) for step in range(1, experts)]
    in_grad = run(
        functools.partial(scatter_body, fold),
        shape((tokens, features)),
        [VMEM] * (fold + experts),
        4 * experts * CAP * tokens * features,
        2 * tokens * features,
        *picks,
        *returned,
        out_spec=HBM,
        scratch=(
            pltpu.VMEM((experts * fold * CAP, features // fold), F32),
            pltpu.VMEM((tokens, features), BF16),
            dma((fold * len(column_spans(features // fold)),)),
        ),
    )
    return (in_grad, grad_gate, grad_up)


def solution(mesh):
    placed = (
        P("expert", "dp"),
        P("expert", "dp"),
        P("expert", None),
        P("expert", None),
        P("dp", "expert"),
        P("dp", "expert"),
        P("expert", "dp"),
    )
    return jax.shard_map(
        per_device,
        mesh=mesh,
        in_specs=placed,
        out_specs=(P("expert", "dp"), P("dp", "expert"), P("dp", "expert")),
        check_vma=False,
    )
```

```python
import functools

import jax
import jax.numpy as jnp
from jax import lax
from jax.experimental import pallas as pl
from jax.experimental.pallas import tpu as pltpu
from jax.sharding import PartitionSpec as P

HSPLIT = 4
CAP = 12
F32 = jnp.float32
BF16 = jnp.bfloat16
VMEM = pl.BlockSpec(memory_space=pltpu.VMEM)
HBM = pl.BlockSpec(memory_space=pltpu.HBM)
ANY = pl.BlockSpec(memory_space=pl.ANY)


def shape(dims, dtype=BF16):
    return jax.ShapeDtypeStruct(dims, dtype)


def run(body, outs, specs, flops, nbytes, *args, out_spec=VMEM, scratch=()):
    return pl.pallas_call(
        body,
        out_shape=outs,
        in_specs=specs,
        out_specs=out_spec if isinstance(out_spec, tuple) else jax.tree.map(lambda _: out_spec, outs),
        scratch_shapes=scratch,
        compiler_params=pltpu.CompilerParams(vmem_limit_bytes=40 * 1024 * 1024),
        cost_estimate=pl.CostEstimate(flops=flops, bytes_accessed=nbytes, transcendentals=0),
    )(*args)


def in_hbm(value):
    return pltpu.with_memory_space_constraint(value, pltpu.HBM)


def dot(left, right, left_dim=1, right_dim=0):
    return lax.dot_general(
        left, right, (((left_dim,), (right_dim,)), ((), ())), preferred_element_type=F32
    )


def iota(dims, dim):
    return lax.broadcasted_iota(jnp.int32, dims, dim)


def over_cap(rows):
    return jnp.floor((rows.astype(F32) + 0.5) * (1.0 / CAP)).astype(jnp.int32)


def column_spans(width, size):
    if width % 128:
        return [slice(0, width)]
    return [slice(start, min(start + size, width)) for start in range(0, width, size)]


def core_columns(width, far):
    side = lax.rem(lax.axis_index("dp"), 2)
    side = 1 - side if far else side
    return pl.ds(pl.multiple_of(side * width, width), width)


def fold_of(width):
    return 2 if width % 256 == 0 else 1


def pick_body(experts, fold, ids_hbm, gates_hbm, grads_hbm, inputs_hbm, *refs):
    picks, pieces = refs[:fold], refs[fold : fold + experts]
    ids, gates, grads, inputs, sems = refs[fold + experts :]
    spans = column_spans(grads.shape[1], 512)
    moves = [(ids_hbm, ids), (gates_hbm, gates)]
    for span in spans:
        moves.append((inputs_hbm.at[:, span], inputs.at[:, span]))
        moves.append((grads_hbm.at[:, span], grads.at[:, span]))
    loads = [
        pltpu.make_async_copy(source, target, sems.at[place])
        for place, (source, target) in enumerate(moves)
    ]
    for load in loads:
        load.start()
    tokens = ids.shape[1]
    padded = max(8, experts)
    group = lax.div(lax.axis_index("expert"), HSPLIT)
    earlier = (iota((tokens, tokens), 0) < iota((tokens, tokens), 1)).astype(F32).astype(BF16)
    loads[0].wait()
    loads[1].wait()
    expert_ids = ids[...]
    route_gates = gates[...]
    match_rows = jnp.zeros((padded, tokens), F32)
    matches = []
    token_gates = []
    for step in range(experts):
        hits = expert_ids == lax.rem(group + step, experts)
        match = jnp.sum(hits.astype(F32), axis=0, keepdims=True)
        matches.append(match)
        token_gates.append(jnp.sum(jnp.where(hits, route_gates, 0.0), axis=0, keepdims=True))
        match_rows = jnp.where(iota((padded, tokens), 0) == step, match, match_rows)
    counts = dot(match_rows.astype(BF16), earlier)
    slots = [
        jnp.where(matches[step] > 0.0, counts[step : step + 1, :], -1.0e6)
        for step in range(experts)
    ]

    def chosen(rows, offset):
        places = (iota((rows, tokens), 0) - offset).astype(F32)
        return [(places == slots[step]).astype(F32) for step in range(experts)]

    input_picks = chosen(2 * CAP, 0)
    grad_picks = chosen(2 * CAP, CAP)
    slot_gates = [
        jnp.sum(hit * gate, axis=1, keepdims=True) for hit, gate in zip(grad_picks, token_gates)
    ]
    gate_column = jnp.concatenate(slot_gates, axis=0)
    input_picks = jnp.concatenate(input_picks, axis=0)
    grad_picks = jnp.concatenate(grad_picks, axis=0)
    if fold == 2:
        picks[0][...] = input_picks.astype(BF16)
        picks[1][...] = grad_picks.astype(BF16)
    else:
        picks[0][...] = jnp.concatenate(chosen(CAP, 0), axis=0).astype(BF16)
    input_picks = input_picks.astype(BF16)
    grad_picks = grad_picks.astype(BF16)
    for place, span in enumerate(spans):
        loads[2 + 2 * place].wait()
        total = dot(input_picks, inputs[:, span])
        loads[3 + 2 * place].wait()
        total = total + dot(grad_picks, grads[:, span]) * gate_column
        for step in range(experts):
            rows = slice(step * 2 * CAP, (step + 1) * 2 * CAP)
            pieces[step][:, span] = total[rows].astype(BF16)


def load_body(parts, after, *refs):
    hbm, (w_gate, w_up, down_across, w_down, sems) = refs[:3], refs[3:]
    loads = []
    for source, target in zip((hbm[2], hbm[0], hbm[1]), (w_down, w_gate, w_up)):
        depth = source.shape[0] // parts
        for part in range(parts):
            rows = slice(part * depth, (part + 1) * depth)
            loads.append(
                pltpu.make_async_copy(source.at[rows], target.at[rows], sems.at[len(loads)])
            )
    for load in loads:
        load.start()
    for load in loads[:parts]:
        load.wait()
    down_across[...] = w_down[...].T
    for load in loads[parts:]:
        load.wait()


def take_rows(offset, pieces):
    rows = []
    for ref in pieces[::-1]:
        piece = ref[...].astype(F32)
        for place in range(offset, piece.shape[0], 2 * CAP):
            rows.append(piece[place : place + CAP])
    return jnp.concatenate(rows, axis=0).astype(BF16)


def gate_body(w_gate, *refs):
    pieces, (rows_out, keep, send) = refs[:-3], refs[-3:]
    half = w_gate.shape[1] // 2
    rows = take_rows(0, pieces)
    rows_out[...] = rows
    for target, far in ((send, True), (keep, False)):
        target[...] = dot(rows, w_gate[:, core_columns(half, far)]).astype(BF16)


def rest_body(w_up, down_across, rows_ref, *refs):
    pieces, (keep, send) = refs[:-2], refs[-2:]
    half = w_up.shape[1] // 2
    rows = rows_ref[...]
    grads = take_rows(CAP, pieces)
    for target, far in ((send, True), (keep, False)):
        columns = core_columns(half, far)
        target[:, :half] = dot(rows, w_up[:, columns]).astype(BF16)
        target[:, half:] = dot(grads, down_across[:, columns]).astype(BF16)


def transpose_body(after, rows_ref, w_gate, w_up, rows_across, gate_across, up_across):
    rows = rows_ref[...]
    count = rows.shape[0]
    same = (iota((count, count), 0) == iota((count, count), 1)).astype(F32).astype(BF16)
    rows_across[...] = dot(rows, same, 0, 0).astype(BF16)
    gate_across[...] = w_gate[...].T
    up_across[...] = w_up[...].T


def core_sum_body(own, other, *refs):
    refs[-1][...] = (own[...].astype(F32) + other[...].astype(F32)).astype(BF16)


def slope_body(own, other, slope, value):
    gate_pre = own[...].astype(F32) + other[...].astype(F32)
    sigma = jax.nn.sigmoid(gate_pre)
    slope[...] = sigma * (1.0 + gate_pre * (1.0 - sigma))
    value[...] = gate_pre * sigma


def activate_body(after, slope, value, rest_own, rest_far, acts):
    half = slope.shape[1]
    rest = rest_own[...].astype(F32) + rest_far[...].astype(F32)
    up_pre = rest[:, :half]
    hidden_grad = rest[:, half:]
    acts[:, :half] = (hidden_grad * up_pre * slope[...]).astype(BF16)
    acts[:, half:] = (hidden_grad * value[...]).astype(BF16)


def fold_rows(rows, fold):
    width = rows.shape[1] // fold
    return [
        jnp.concatenate(
            [rows[place : place + CAP, part * width : (part + 1) * width] for part in range(fold)],
            axis=0,
        )
        for place in range(0, rows.shape[0], CAP)
    ]


def back_part(gate_across, up_across, acts, sibling):
    half = gate_across.shape[0] // 2
    units = core_columns(half, sibling)
    part = dot(acts[:, :half], gate_across[units, :])
    return part + dot(acts[:, half:], up_across[units, :])


def back_own_body(gate_across, up_across, acts, total):
    total[...] = back_part(gate_across, up_across, acts, False)


def back_far_body(gate_across, up_across, acts, own, *outs):
    count = outs[0].shape[0]
    total = own[...] + back_part(gate_across, up_across, acts, True)
    for place, out in enumerate(outs):
        out[...] = total[place * count : (place + 1) * count].astype(BF16)


def weight_body(which, chunks, after, rows_ref, acts_own, acts_far, out, token, tile, sems):
    token[...] = jnp.zeros_like(token)
    half = out.shape[1] // 2
    depth = out.shape[0] // chunks
    columns = slice(which * half, (which + 1) * half)
    stores = []
    for chunk in range(chunks):
        span = slice(chunk * depth, (chunk + 1) * depth)
        rows = rows_ref[span, :]
        for acts, far in ((acts_own, False), (acts_far, True)):
            tile[span, core_columns(half, far)] = dot(rows, acts[:, columns]).astype(BF16)
        stores.append(pltpu.make_async_copy(tile.at[span], out.at[span], sems.at[chunk]))
        stores[-1].start()
    for store in stores:
        store.wait()


def gather_body(fold, experts, after, *refs):
    parts, outs = refs[:HSPLIT], refs[HSPLIT:]
    total = parts[0][...].astype(F32) + parts[1][...].astype(F32)
    total = total + (parts[2][...].astype(F32) + parts[3][...].astype(F32))
    for out, rows in zip(outs, fold_rows(total, fold)):
        out[...] = rows.astype(BF16)


def scatter_body(fold, *refs):
    picks, pieces = refs[:fold], refs[fold:-4]
    out, stack, tile, sems = refs[-4:]
    width = out.shape[1] // fold
    piece = CAP * fold
    for place, ref in enumerate(pieces):
        stack[place * piece : (place + 1) * piece, :] = ref[...].astype(F32)
    returned = stack[...].astype(BF16)
    stores = []
    for part in range(fold):
        for span in column_spans(width, 384):
            target = slice(part * width + span.start, part * width + span.stop)
            tile[:, target] = dot(picks[part][...], returned[:, span], 0, 0).astype(BF16)
            store = pltpu.make_async_copy(
                tile.at[:, target], out.at[:, target], sems.at[len(stores)]
            )
            store.start()
            stores.append(store)
    for store in stores:
        store.wait()


def per_device(out_grad, inputs, expert_ids, gate_weights, w_gate, w_up, w_down):
    devices = lax.axis_size("expert")
    spread = lax.axis_size("dp")
    experts = devices // HSPLIT
    tokens, features = out_grad.shape
    routed = expert_ids.shape[1]
    fold = fold_of(features)
    hidden = w_gate.shape[1]
    half = hidden // 2
    count = devices * CAP
    product = 2 * count * features * hidden
    dma = pltpu.SemaphoreType.DMA

    def to_expert(value, step):
        pairs = [(d, (d + step * HSPLIT) % devices) for d in range(devices)]
        return lax.ppermute(value, "expert", pairs)

    def to_peer(value, flip):
        return lax.ppermute(value, "expert", [(d, d ^ flip) for d in range(devices)])

    def to_dp(value, flip):
        return lax.ppermute(value, "dp", [(d, d ^ flip) for d in range(spread)])

    picked = run(
        functools.partial(pick_body, experts, fold),
        (shape((experts * fold * CAP, tokens)),) * fold
        + (shape((2 * CAP, features)),) * experts,
        [HBM] * 4,
        8 * experts * CAP * tokens * features,
        4 * tokens * features,
        *(in_hbm(array) for array in (expert_ids.T, gate_weights.T, out_grad, inputs)),
        scratch=(
            pltpu.VMEM((routed, tokens), jnp.int32),
            pltpu.VMEM((routed, tokens), F32),
            pltpu.VMEM((tokens, features), BF16),
            pltpu.VMEM((tokens, features), BF16),
            dma((2 + 2 * len(column_spans(features, 512)),)),
        ),
    )
    picks, own = picked[:fold], picked[fold:]
    gate_here, up_here, down_across = run(
        functools.partial(load_body, 4),
        tuple(pltpu.VMEM(dims, BF16) for dims in (w_gate.shape, w_up.shape, w_down.shape[::-1])),
        [ANY] + [HBM] * 3,
        0,
        6 * features * hidden,
        picks[0],
        *(in_hbm(weight) for weight in (w_gate, w_up, w_down)),
        scratch=(pltpu.VMEM(w_down.shape, BF16), dma((12,))),
    )

    away = [to_expert(own[step], step) for step in range(1, experts)]
    near = [own[0]] + [to_peer(own[0], flip) for flip in range(1, HSPLIT)]
    away = away[0] if len(away) == 1 else jnp.concatenate(away, axis=0)
    far = [away] + [to_peer(away, flip) for flip in range(1, HSPLIT)]
    pieces = [array for pair in zip(near, far) for array in pair][::-1]

    rows_input, gate_keep, gate_send = run(
        gate_body,
        (shape((count, features)), shape((count, half)), shape((count, half))),
        [VMEM] * (1 + len(pieces)),
        product,
        2 * features * hidden,
        gate_here,
        *pieces,
    )

    rest_keep, rest_send = run(
        rest_body,
        (shape((count, hidden)),) * 2,
        [VMEM] * (3 + len(pieces)),
        0,
        0,
        up_here,
        down_across,
        rows_input,
        *pieces,
    )
    def core_sum(keep, send, flops, *after):
        return run(
            core_sum_body,
            shape(keep.shape),
            [VMEM] * 2 + [ANY] * len(after),
            flops,
            0,
            keep,
            to_dp(send, 1),
            *after,
        )

    def spread_sum(total):
        flip = 2
        other = jnp.zeros_like(total)
        while flip < spread:
            other = to_dp(total, flip)
            flip *= 2
            if flip < spread:
                total = (total.astype(F32) + other.astype(F32)).astype(BF16)
        return total, other

    gate_sum = core_sum(gate_keep, gate_send, 8 * product)
    gate_own, gate_far = spread_sum(gate_sum)
    slope, value = run(
        slope_body,
        (shape((count, half), F32),) * 2,
        [VMEM] * 2,
        8 * product,
        0,
        gate_own,
        gate_far,
    )
    rest_own, rest_far = spread_sum(core_sum(rest_keep, rest_send, 0, gate_sum))
    rows_across, gate_across, up_across = run(
        transpose_body,
        (shape((features, count)),) + (shape((hidden, features)),) * 2,
        [ANY] + [VMEM] * 3,
        0,
        0,
        slope,
        rows_input,
        gate_here,
        up_here,
    )
    acts = run(
        activate_body,
        shape((count, hidden)),
        [ANY] + [VMEM] * 4,
        20 * count * half,
        10 * count * half,
        rows_across,
        slope,
        value,
        rest_own,
        rest_far,
    )
    acts_far = to_dp(acts, 1)
    back_own = run(
        back_own_body,
        shape((count, features), F32),
        [VMEM] * 3,
        product,
        2 * features * hidden,
        gate_across,
        up_across,
        acts,
    )
    back = run(
        back_far_body,
        (shape((count // HSPLIT, features)),) * HSPLIT,
        [VMEM] * 4,
        product,
        2 * features * hidden,
        gate_across,
        up_across,
        acts_far,
        back_own,
    )

    def weight_grad(which, after):
        chunks = features // 256 if features % 256 == 0 else 2
        return run(
            functools.partial(weight_body, which, chunks),
            (shape((features, hidden)), shape((8, 128), F32)),
            [ANY] + [VMEM] * 3,
            0,
            0,
            after,
            rows_across,
            acts,
            acts_far,
            out_spec=(HBM, VMEM),
            scratch=(pltpu.VMEM((features, hidden), BF16), dma((chunks,))),
        )

    grad_gate, token = weight_grad(0, back[0])
    summed = run(
        functools.partial(gather_body, fold, experts),
        (shape((CAP * fold, features // fold)),) * experts,
        [ANY] + [VMEM] * HSPLIT,
        0,
        0,
        token,
        *(to_peer(back[flip], flip) for flip in range(HSPLIT - 1, 0, -1)),
        back[0],
    )
    grad_up, _ = weight_grad(1, summed[0])
    returned = [summed[0]] + [to_expert(summed[step], experts - step) for step in range(1, experts)]
    in_grad = run(
        functools.partial(scatter_body, fold),
        shape((tokens, features)),
        [VMEM] * (fold + experts),
        4 * experts * CAP * tokens * features,
        2 * tokens * features,
        *picks,
        *returned,
        out_spec=HBM,
        scratch=(
            pltpu.VMEM((experts * fold * CAP, features // fold), F32),
            pltpu.VMEM((tokens, features), BF16),
            dma((fold * len(column_spans(features // fold, 384)),)),
        ),
    )
    return (in_grad, grad_gate, grad_up)


def solution(mesh):
    placed = (
        P("expert", "dp"),
        P("expert", "dp"),
        P("expert", None),
        P("expert", None),
        P("dp", "expert"),
        P("dp", "expert"),
        P("expert", "dp"),
    )
    return jax.shard_map(
        per_device,
        mesh=mesh,
        in_specs=placed,
        out_specs=(P("expert", "dp"), P("dp", "expert"), P("dp", "expert")),
        check_vma=False,
    )
```

```python
import functools

import jax
import jax.numpy as jnp
from jax import lax
from jax.experimental import pallas as pl
from jax.experimental.pallas import tpu as pltpu
from jax.sharding import PartitionSpec as P

HSPLIT = 4
CAP = 12
F32 = jnp.float32
BF16 = jnp.bfloat16
VMEM = pl.BlockSpec(memory_space=pltpu.VMEM)
HBM = pl.BlockSpec(memory_space=pltpu.HBM)
ANY = pl.BlockSpec(memory_space=pl.ANY)


def shape(dims, dtype=BF16):
    return jax.ShapeDtypeStruct(dims, dtype)


def run(body, outs, specs, flops, nbytes, *args, out_spec=VMEM, scratch=()):
    return pl.pallas_call(
        body,
        out_shape=outs,
        in_specs=specs,
        out_specs=out_spec if isinstance(out_spec, tuple) else jax.tree.map(lambda _: out_spec, outs),
        scratch_shapes=scratch,
        compiler_params=pltpu.CompilerParams(vmem_limit_bytes=40 * 1024 * 1024),
        cost_estimate=pl.CostEstimate(flops=flops, bytes_accessed=nbytes, transcendentals=0),
    )(*args)


def in_hbm(value):
    return pltpu.with_memory_space_constraint(value, pltpu.HBM)


def dot(left, right, left_dim=1, right_dim=0):
    return lax.dot_general(
        left, right, (((left_dim,), (right_dim,)), ((), ())), preferred_element_type=F32
    )


def iota(dims, dim):
    return lax.broadcasted_iota(jnp.int32, dims, dim)


def over_cap(rows):
    return jnp.floor((rows.astype(F32) + 0.5) * (1.0 / CAP)).astype(jnp.int32)


def column_spans(width):
    whole = width // 128 * 128
    if whole != width or width < 512:
        return [slice(0, width)]
    middle = width // 256 * 128
    return [slice(0, middle), slice(middle, width)]


def core_columns(width, far):
    side = lax.rem(lax.axis_index("dp"), 2)
    side = 1 - side if far else side
    return pl.ds(pl.multiple_of(side * width, width), width)


def fold_of(width):
    return 2 if width % 256 == 0 else 1


def pick_body(experts, fold, ids_hbm, gates_hbm, grads_hbm, inputs_hbm, *refs):
    picks, pieces = refs[:fold], refs[fold : fold + experts]
    ids, gates, grads, inputs, sems = refs[fold + experts :]
    spans = column_spans(grads.shape[1])
    moves = [(ids_hbm, ids), (gates_hbm, gates)]
    for span in spans:
        moves.append((inputs_hbm.at[:, span], inputs.at[:, span]))
        moves.append((grads_hbm.at[:, span], grads.at[:, span]))
    loads = [
        pltpu.make_async_copy(source, target, sems.at[place])
        for place, (source, target) in enumerate(moves)
    ]
    for load in loads:
        load.start()
    tokens = ids.shape[1]
    padded = max(8, experts)
    group = lax.div(lax.axis_index("expert"), HSPLIT)
    earlier = (iota((tokens, tokens), 0) < iota((tokens, tokens), 1)).astype(F32).astype(BF16)
    loads[0].wait()
    loads[1].wait()
    expert_ids = ids[...]
    route_gates = gates[...]
    match_rows = jnp.zeros((padded, tokens), F32)
    matches = []
    token_gates = []
    for step in range(experts):
        hits = expert_ids == lax.rem(group + step, experts)
        match = jnp.sum(hits.astype(F32), axis=0, keepdims=True)
        matches.append(match)
        token_gates.append(jnp.sum(jnp.where(hits, route_gates, 0.0), axis=0, keepdims=True))
        match_rows = jnp.where(iota((padded, tokens), 0) == step, match, match_rows)
    counts = dot(match_rows.astype(BF16), earlier)
    slots = [
        jnp.where(matches[step] > 0.0, counts[step : step + 1, :], -1.0e6)
        for step in range(experts)
    ]

    def chosen(rows, offset):
        places = (iota((rows, tokens), 0) - offset).astype(F32)
        return [(places == slots[step]).astype(F32) for step in range(experts)]

    input_picks = chosen(2 * CAP, 0)
    grad_picks = chosen(2 * CAP, CAP)
    slot_gates = [
        jnp.sum(hit * gate, axis=1, keepdims=True) for hit, gate in zip(grad_picks, token_gates)
    ]
    gate_column = jnp.concatenate(slot_gates, axis=0)
    input_picks = jnp.concatenate(input_picks, axis=0)
    grad_picks = jnp.concatenate(grad_picks, axis=0)
    if fold == 2:
        picks[0][...] = input_picks.astype(BF16)
        picks[1][...] = grad_picks.astype(BF16)
    else:
        picks[0][...] = jnp.concatenate(chosen(CAP, 0), axis=0).astype(BF16)
    input_picks = input_picks.astype(BF16)
    grad_picks = grad_picks.astype(BF16)
    for place, span in enumerate(spans):
        loads[2 + 2 * place].wait()
        total = dot(input_picks, inputs[:, span])
        loads[3 + 2 * place].wait()
        total = total + dot(grad_picks, grads[:, span]) * gate_column
        for step in range(experts):
            rows = slice(step * 2 * CAP, (step + 1) * 2 * CAP)
            pieces[step][:, span] = total[rows].astype(BF16)


def load_body(parts, after, *refs):
    hbm, (w_gate, w_up, down_across, w_down, sems) = refs[:3], refs[3:]
    loads = []
    for source, target in zip((hbm[2], hbm[0], hbm[1]), (w_down, w_gate, w_up)):
        depth = source.shape[0] // parts
        for part in range(parts):
            rows = slice(part * depth, (part + 1) * depth)
            loads.append(
                pltpu.make_async_copy(source.at[rows], target.at[rows], sems.at[len(loads)])
            )
    for load in loads:
        load.start()
    for load in loads[:parts]:
        load.wait()
    down_across[...] = w_down[...].T
    for load in loads[parts:]:
        load.wait()


def take_rows(offset, pieces):
    rows = []
    for ref in pieces[::-1]:
        piece = ref[...].astype(F32)
        for place in range(offset, piece.shape[0], 2 * CAP):
            rows.append(piece[place : place + CAP])
    return jnp.concatenate(rows, axis=0).astype(BF16)


def forward_body(w_gate, w_up, *refs):
    pieces, (rows_out, keep, send) = refs[:-3], refs[-3:]
    half = w_gate.shape[1] // 2
    rows = take_rows(0, pieces)
    rows_out[...] = rows
    for target, far in ((send, True), (keep, False)):
        columns = core_columns(half, far)
        target[:, :half] = dot(rows, w_gate[:, columns]).astype(BF16)
        target[:, half:] = dot(rows, w_up[:, columns]).astype(BF16)


def hidden_body(down_across, *refs):
    pieces, (keep, send) = refs[:-2], refs[-2:]
    half = down_across.shape[1] // 2
    rows = take_rows(CAP, pieces)
    for target, far in ((send, True), (keep, False)):
        target[...] = dot(rows, down_across[:, core_columns(half, far)]).astype(BF16)


def transpose_body(after, rows_ref, w_gate, w_up, rows_across, gate_across, up_across):
    rows = rows_ref[...]
    count = rows.shape[0]
    same = (iota((count, count), 0) == iota((count, count), 1)).astype(F32).astype(BF16)
    rows_across[...] = dot(rows, same, 0, 0).astype(BF16)
    gate_across[...] = w_gate[...].T
    up_across[...] = w_up[...].T


def activate_body(after, pre_own, pre_far, hid_own, hid_far, acts):
    half = hid_own.shape[1]
    pre = pre_own[...].astype(F32) + pre_far[...].astype(F32)
    hidden_grad = hid_own[...].astype(F32) + hid_far[...].astype(F32)
    gate_pre = pre[:, :half]
    up_pre = pre[:, half:]
    sigma = jax.nn.sigmoid(gate_pre)
    acts[:, :half] = (hidden_grad * up_pre * sigma * (1.0 + gate_pre * (1.0 - sigma))).astype(BF16)
    acts[:, half:] = (hidden_grad * gate_pre * sigma).astype(BF16)


def fold_rows(rows, fold):
    width = rows.shape[1] // fold
    return [
        jnp.concatenate(
            [rows[place : place + CAP, part * width : (part + 1) * width] for part in range(fold)],
            axis=0,
        )
        for place in range(0, rows.shape[0], CAP)
    ]


def back_part(gate_across, up_across, acts, sibling):
    half = gate_across.shape[0] // 2
    units = core_columns(half, sibling)
    part = dot(acts[:, :half], gate_across[units, :])
    return part + dot(acts[:, half:], up_across[units, :])


def back_own_body(gate_across, up_across, acts, total):
    total[...] = back_part(gate_across, up_across, acts, False)


def back_far_body(gate_across, up_across, acts, own, *outs):
    count = outs[0].shape[0]
    total = own[...] + back_part(gate_across, up_across, acts, True)
    for place, out in enumerate(outs):
        out[...] = total[place * count : (place + 1) * count].astype(BF16)


def weight_body(which, chunks, after, rows_ref, acts_own, acts_far, out, token, tile, sems):
    token[...] = jnp.zeros_like(token)
    half = out.shape[1] // 2
    depth = out.shape[0] // chunks
    columns = slice(which * half, (which + 1) * half)
    stores = []
    for chunk in range(chunks):
        span = slice(chunk * depth, (chunk + 1) * depth)
        rows = rows_ref[span, :]
        for acts, far in ((acts_own, False), (acts_far, True)):
            tile[span, core_columns(half, far)] = dot(rows, acts[:, columns]).astype(BF16)
        stores.append(pltpu.make_async_copy(tile.at[span], out.at[span], sems.at[chunk]))
        stores[-1].start()
    for store in stores:
        store.wait()


def gather_body(fold, experts, after, *refs):
    parts, outs = refs[:HSPLIT], refs[HSPLIT:]
    total = parts[0][...].astype(F32) + parts[1][...].astype(F32)
    total = total + (parts[2][...].astype(F32) + parts[3][...].astype(F32))
    for out, rows in zip(outs, fold_rows(total, fold)):
        out[...] = rows.astype(BF16)


def scatter_body(fold, *refs):
    picks, pieces = refs[:fold], refs[fold:-4]
    out, stack, tile, sems = refs[-4:]
    width = out.shape[1] // fold
    piece = CAP * fold
    for place, ref in enumerate(pieces):
        stack[place * piece : (place + 1) * piece, :] = ref[...].astype(F32)
    returned = stack[...].astype(BF16)
    stores = []
    for part in range(fold):
        for span in column_spans(width):
            target = slice(part * width + span.start, part * width + span.stop)
            tile[:, target] = dot(picks[part][...], returned[:, span], 0, 0).astype(BF16)
            store = pltpu.make_async_copy(
                tile.at[:, target], out.at[:, target], sems.at[len(stores)]
            )
            store.start()
            stores.append(store)
    for store in stores:
        store.wait()


def per_device(out_grad, inputs, expert_ids, gate_weights, w_gate, w_up, w_down):
    devices = lax.axis_size("expert")
    spread = lax.axis_size("dp")
    experts = devices // HSPLIT
    tokens, features = out_grad.shape
    routed = expert_ids.shape[1]
    fold = fold_of(features)
    hidden = w_gate.shape[1]
    half = hidden // 2
    count = devices * CAP
    product = 2 * count * features * hidden
    dma = pltpu.SemaphoreType.DMA

    def to_expert(value, step):
        pairs = [(d, (d + step * HSPLIT) % devices) for d in range(devices)]
        return lax.ppermute(value, "expert", pairs)

    def to_peer(value, flip):
        return lax.ppermute(value, "expert", [(d, d ^ flip) for d in range(devices)])

    def to_dp(value, flip):
        return lax.ppermute(value, "dp", [(d, d ^ flip) for d in range(spread)])

    picked = run(
        functools.partial(pick_body, experts, fold),
        (shape((experts * fold * CAP, tokens)),) * fold
        + (shape((2 * CAP, features)),) * experts,
        [HBM] * 4,
        8 * experts * CAP * tokens * features,
        4 * tokens * features,
        *(in_hbm(array) for array in (expert_ids.T, gate_weights.T, out_grad, inputs)),
        scratch=(
            pltpu.VMEM((routed, tokens), jnp.int32),
            pltpu.VMEM((routed, tokens), F32),
            pltpu.VMEM((tokens, features), BF16),
            pltpu.VMEM((tokens, features), BF16),
            dma((2 + 2 * len(column_spans(features)),)),
        ),
    )
    picks, own = picked[:fold], picked[fold:]
    gate_here, up_here, down_across = run(
        functools.partial(load_body, 4),
        tuple(pltpu.VMEM(dims, BF16) for dims in (w_gate.shape, w_up.shape, w_down.shape[::-1])),
        [ANY] + [HBM] * 3,
        0,
        6 * features * hidden,
        picks[0],
        *(in_hbm(weight) for weight in (w_gate, w_up, w_down)),
        scratch=(pltpu.VMEM(w_down.shape, BF16), dma((12,))),
    )

    away = [to_expert(own[step], step) for step in range(1, experts)]
    near = [own[0]] + [to_peer(own[0], flip) for flip in range(1, HSPLIT)]
    away = away[0] if len(away) == 1 else jnp.concatenate(away, axis=0)
    far = [away] + [to_peer(away, flip) for flip in range(1, HSPLIT)]
    pieces = [array for pair in zip(near, far) for array in pair][::-1]

    rows_input, pre_keep, pre_send = run(
        forward_body,
        (shape((count, features)), shape((count, hidden)), shape((count, hidden))),
        [VMEM] * (2 + len(pieces)),
        2 * product,
        4 * features * hidden,
        gate_here,
        up_here,
        *pieces,
    )

    def spread_sum(keep, send):
        near = (keep.astype(F32) + to_dp(send, 1).astype(F32)).astype(BF16)
        flip = 2
        far = jnp.zeros_like(near)
        while flip < spread:
            far = to_dp(near, flip)
            flip *= 2
            if flip < spread:
                near = (near.astype(F32) + far.astype(F32)).astype(BF16)
        return near, far

    pre_own, pre_far = spread_sum(pre_keep, pre_send)
    hid_keep, hid_send = run(
        hidden_body,
        (shape((count, half)), shape((count, half))),
        [VMEM] * (1 + len(pieces)),
        product,
        2 * features * hidden,
        down_across,
        *pieces,
    )
    hid_own, hid_far = spread_sum(hid_keep, hid_send)
    rows_across, gate_across, up_across = run(
        transpose_body,
        (shape((features, count)),) + (shape((hidden, features)),) * 2,
        [ANY] + [VMEM] * 3,
        0,
        0,
        hid_own,
        rows_input,
        gate_here,
        up_here,
    )
    acts = run(
        activate_body,
        shape((count, hidden)),
        [ANY] + [VMEM] * 4,
        20 * count * half,
        10 * count * half,
        rows_across,
        pre_own,
        pre_far,
        hid_own,
        hid_far,
    )
    acts_far = to_dp(acts, 1)
    back_own = run(
        back_own_body,
        shape((count, features), F32),
        [VMEM] * 3,
        product,
        2 * features * hidden,
        gate_across,
        up_across,
        acts,
    )
    back = run(
        back_far_body,
        (shape((count // HSPLIT, features)),) * HSPLIT,
        [VMEM] * 4,
        product,
        2 * features * hidden,
        gate_across,
        up_across,
        acts_far,
        back_own,
    )

    def weight_grad(which, after):
        chunks = features // 256 if features % 256 == 0 else 2
        return run(
            functools.partial(weight_body, which, chunks),
            (shape((features, hidden)), shape((8, 128), F32)),
            [ANY] + [VMEM] * 3,
            0,
            0,
            after,
            rows_across,
            acts,
            acts_far,
            out_spec=(HBM, VMEM),
            scratch=(pltpu.VMEM((features, hidden), BF16), dma((chunks,))),
        )

    grad_gate, token = weight_grad(0, back[0])
    grad_up, token = weight_grad(1, token)
    summed = run(
        functools.partial(gather_body, fold, experts),
        (shape((CAP * fold, features // fold)),) * experts,
        [ANY] + [VMEM] * HSPLIT,
        0,
        0,
        token,
        *(to_peer(back[flip], flip) for flip in range(HSPLIT - 1, 0, -1)),
        back[0],
    )
    returned = [summed[0]] + [to_expert(summed[step], experts - step) for step in range(1, experts)]
    in_grad = run(
        functools.partial(scatter_body, fold),
        shape((tokens, features)),
        [VMEM] * (fold + experts),
        4 * experts * CAP * tokens * features,
        2 * tokens * features,
        *picks,
        *returned,
        out_spec=HBM,
        scratch=(
            pltpu.VMEM((experts * fold * CAP, features // fold), F32),
            pltpu.VMEM((tokens, features), BF16),
            dma((fold * len(column_spans(features // fold)),)),
        ),
    )
    return (in_grad, grad_gate, grad_up)


def solution(mesh):
    placed = (
        P("expert", "dp"),
        P("expert", "dp"),
        P("expert", None),
        P("expert", None),
        P("dp", "expert"),
        P("dp", "expert"),
        P("expert", "dp"),
    )
    return jax.shard_map(
        per_device,
        mesh=mesh,
        in_specs=placed,
        out_specs=(P("expert", "dp"), P("dp", "expert"), P("dp", "expert")),
        check_vma=False,
    )
```

```python
import functools

import jax
import jax.numpy as jnp
from jax import lax
from jax.experimental import pallas as pl
from jax.experimental.pallas import tpu as pltpu
from jax.sharding import PartitionSpec as P

HSPLIT = 4
CAP = 12
F32 = jnp.float32
BF16 = jnp.bfloat16
VMEM = pl.BlockSpec(memory_space=pltpu.VMEM)
HBM = pl.BlockSpec(memory_space=pltpu.HBM)
ANY = pl.BlockSpec(memory_space=pl.ANY)


def shape(dims, dtype=BF16):
    return jax.ShapeDtypeStruct(dims, dtype)


def run(body, outs, specs, flops, nbytes, *args, out_spec=VMEM, scratch=()):
    return pl.pallas_call(
        body,
        out_shape=outs,
        in_specs=specs,
        out_specs=out_spec if isinstance(out_spec, tuple) else jax.tree.map(lambda _: out_spec, outs),
        scratch_shapes=scratch,
        compiler_params=pltpu.CompilerParams(vmem_limit_bytes=40 * 1024 * 1024),
        cost_estimate=pl.CostEstimate(flops=flops, bytes_accessed=nbytes, transcendentals=0),
    )(*args)


def in_hbm(value):
    return pltpu.with_memory_space_constraint(value, pltpu.HBM)


def dot(left, right, left_dim=1, right_dim=0):
    return lax.dot_general(
        left, right, (((left_dim,), (right_dim,)), ((), ())), preferred_element_type=F32
    )


def iota(dims, dim):
    return lax.broadcasted_iota(jnp.int32, dims, dim)


def over_cap(rows):
    return jnp.floor((rows.astype(F32) + 0.5) * (1.0 / CAP)).astype(jnp.int32)


def column_spans(width):
    whole = width // 128 * 128
    if whole != width or width < 512:
        return [slice(0, width)]
    middle = width // 256 * 128
    return [slice(0, middle), slice(middle, width)]


def core_columns(width, far):
    side = lax.rem(lax.axis_index("dp"), 2)
    side = 1 - side if far else side
    return pl.ds(pl.multiple_of(side * width, width), width)


def fold_of(width):
    return 2 if width % 256 == 0 else 1


def pick_body(experts, fold, ids_hbm, gates_hbm, grads_hbm, inputs_hbm, *refs):
    picks, pieces = refs[:fold], refs[fold : fold + experts]
    ids, gates, grads, inputs, sems = refs[fold + experts :]
    spans = column_spans(grads.shape[1])
    moves = [(ids_hbm, ids), (gates_hbm, gates)]
    for span in spans:
        moves.append((inputs_hbm.at[:, span], inputs.at[:, span]))
        moves.append((grads_hbm.at[:, span], grads.at[:, span]))
    loads = [
        pltpu.make_async_copy(source, target, sems.at[place])
        for place, (source, target) in enumerate(moves)
    ]
    for load in loads:
        load.start()
    tokens = ids.shape[1]
    padded = max(8, experts)
    group = lax.div(lax.axis_index("expert"), HSPLIT)
    earlier = (iota((tokens, tokens), 0) < iota((tokens, tokens), 1)).astype(F32).astype(BF16)
    loads[0].wait()
    loads[1].wait()
    expert_ids = ids[...]
    route_gates = gates[...]
    match_rows = jnp.zeros((padded, tokens), F32)
    matches = []
    token_gates = []
    for step in range(experts):
        hits = expert_ids == lax.rem(group + step, experts)
        match = jnp.sum(hits.astype(F32), axis=0, keepdims=True)
        matches.append(match)
        token_gates.append(jnp.sum(jnp.where(hits, route_gates, 0.0), axis=0, keepdims=True))
        match_rows = jnp.where(iota((padded, tokens), 0) == step, match, match_rows)
    counts = dot(match_rows.astype(BF16), earlier)
    slots = [
        jnp.where(matches[step] > 0.0, counts[step : step + 1, :], -1.0e6)
        for step in range(experts)
    ]

    def chosen(rows, offset):
        places = (iota((rows, tokens), 0) - offset).astype(F32)
        return [(places == slots[step]).astype(F32) for step in range(experts)]

    input_picks = chosen(2 * CAP, 0)
    grad_picks = chosen(2 * CAP, CAP)
    slot_gates = [
        jnp.sum(hit * gate, axis=1, keepdims=True) for hit, gate in zip(grad_picks, token_gates)
    ]
    gate_column = jnp.concatenate(slot_gates, axis=0)
    input_picks = jnp.concatenate(input_picks, axis=0)
    grad_picks = jnp.concatenate(grad_picks, axis=0)
    if fold == 2:
        picks[0][...] = input_picks.astype(BF16)
        picks[1][...] = grad_picks.astype(BF16)
    else:
        picks[0][...] = jnp.concatenate(chosen(CAP, 0), axis=0).astype(BF16)
    input_picks = input_picks.astype(BF16)
    grad_picks = grad_picks.astype(BF16)
    for place, span in enumerate(spans):
        loads[2 + 2 * place].wait()
        total = dot(input_picks, inputs[:, span])
        loads[3 + 2 * place].wait()
        total = total + dot(grad_picks, grads[:, span]) * gate_column
        for step in range(experts):
            rows = slice(step * 2 * CAP, (step + 1) * 2 * CAP)
            pieces[step][:, span] = total[rows].astype(BF16)


def load_body(parts, after, *refs):
    hbm, (w_gate, w_up, down_across, w_down, sems) = refs[:3], refs[3:]
    loads = []
    for source, target in zip((hbm[2], hbm[0], hbm[1]), (w_down, w_gate, w_up)):
        depth = source.shape[0] // parts
        for part in range(parts):
            rows = slice(part * depth, (part + 1) * depth)
            loads.append(
                pltpu.make_async_copy(source.at[rows], target.at[rows], sems.at[len(loads)])
            )
    for load in loads:
        load.start()
    for load in loads[:parts]:
        load.wait()
    down_across[...] = w_down[...].T
    for load in loads[parts:]:
        load.wait()


def take_rows(offset, pieces):
    rows = []
    for ref in pieces[::-1]:
        piece = ref[...].astype(F32)
        for place in range(offset, piece.shape[0], 2 * CAP):
            rows.append(piece[place : place + CAP])
    return jnp.concatenate(rows, axis=0).astype(BF16)


def pre_part(rows, w_gate, w_up, out, far):
    half = w_gate.shape[1] // 2
    columns = core_columns(half, far)
    out[:, :half] = dot(rows, w_gate[:, columns]).astype(BF16)
    out[:, half:] = dot(rows, w_up[:, columns]).astype(BF16)


def pre_send_body(w_gate, w_up, *refs):
    pieces, (rows_out, send) = refs[:-2], refs[-2:]
    rows = take_rows(0, pieces)
    rows_out[...] = rows
    pre_part(rows, w_gate, w_up, send, True)


def pre_keep_body(after, w_gate, w_up, rows_ref, keep):
    pre_part(rows_ref[...], w_gate, w_up, keep, False)


def hidden_send_body(down_across, *refs):
    pieces, (rows_out, send) = refs[:-2], refs[-2:]
    half = down_across.shape[1] // 2
    rows = take_rows(CAP, pieces)
    rows_out[...] = rows
    send[...] = dot(rows, down_across[:, core_columns(half, True)]).astype(BF16)


def hidden_keep_body(down_across, rows_ref, keep):
    half = down_across.shape[1] // 2
    keep[...] = dot(rows_ref[...], down_across[:, core_columns(half, False)]).astype(BF16)


def transpose_body(after, rows_ref, w_gate, w_up, rows_across, gate_across, up_across):
    rows = rows_ref[...]
    count = rows.shape[0]
    same = (iota((count, count), 0) == iota((count, count), 1)).astype(F32).astype(BF16)
    rows_across[...] = dot(rows, same, 0, 0).astype(BF16)
    gate_across[...] = w_gate[...].T
    up_across[...] = w_up[...].T


def activate_body(after, pre_own, pre_far, hid_own, hid_far, gate_acts, up_acts):
    half = hid_own.shape[1]
    pre = pre_own[...].astype(F32) + pre_far[...].astype(F32)
    hidden_grad = hid_own[...].astype(F32) + hid_far[...].astype(F32)
    gate_pre = pre[:, :half]
    up_pre = pre[:, half:]
    sigma = jax.nn.sigmoid(gate_pre)
    gate_acts[...] = (hidden_grad * up_pre * sigma * (1.0 + gate_pre * (1.0 - sigma))).astype(BF16)
    up_acts[...] = (hidden_grad * gate_pre * sigma).astype(BF16)


def fold_rows(rows, fold):
    width = rows.shape[1] // fold
    return [
        jnp.concatenate(
            [rows[place : place + CAP, part * width : (part + 1) * width] for part in range(fold)],
            axis=0,
        )
        for place in range(0, rows.shape[0], CAP)
    ]


def back_part(across, acts, sibling):
    return dot(acts[...], across[core_columns(across.shape[0] // 2, sibling), :])


def back_own_body(gate_across, up_across, gate_acts, up_acts, total):
    total[...] = back_part(gate_across, gate_acts, False) + back_part(up_across, up_acts, False)


def back_gate_body(gate_across, gate_acts, own, total):
    total[...] = own[...] + back_part(gate_across, gate_acts, True)


def back_up_body(up_across, up_acts, own, *outs):
    count = outs[0].shape[0]
    total = own[...] + back_part(up_across, up_acts, True)
    for place, out in enumerate(outs):
        out[...] = total[place * count : (place + 1) * count].astype(BF16)


def weight_body(chunks, after, rows_ref, acts_own, acts_far, out, token, tile, sems):
    token[...] = jnp.zeros_like(token)
    half = out.shape[1] // 2
    depth = out.shape[0] // chunks
    stores = []
    for chunk in range(chunks):
        span = slice(chunk * depth, (chunk + 1) * depth)
        rows = rows_ref[span, :]
        for acts, far in ((acts_own, False), (acts_far, True)):
            tile[span, core_columns(half, far)] = dot(rows, acts[...]).astype(BF16)
        stores.append(pltpu.make_async_copy(tile.at[span], out.at[span], sems.at[chunk]))
        stores[-1].start()
    for store in stores:
        store.wait()


def gather_body(fold, experts, after, *refs):
    parts, outs = refs[:HSPLIT], refs[HSPLIT:]
    total = parts[0][...].astype(F32) + parts[1][...].astype(F32)
    total = total + (parts[2][...].astype(F32) + parts[3][...].astype(F32))
    for out, rows in zip(outs, fold_rows(total, fold)):
        out[...] = rows.astype(BF16)


def scatter_body(fold, *refs):
    picks, pieces = refs[:fold], refs[fold:-4]
    out, stack, tile, sems = refs[-4:]
    width = out.shape[1] // fold
    piece = CAP * fold
    for place, ref in enumerate(pieces):
        stack[place * piece : (place + 1) * piece, :] = ref[...].astype(F32)
    returned = stack[...].astype(BF16)
    stores = []
    for part in range(fold):
        for span in column_spans(width):
            target = slice(part * width + span.start, part * width + span.stop)
            tile[:, target] = dot(picks[part][...], returned[:, span], 0, 0).astype(BF16)
            store = pltpu.make_async_copy(
                tile.at[:, target], out.at[:, target], sems.at[len(stores)]
            )
            store.start()
            stores.append(store)
    for store in stores:
        store.wait()


def per_device(out_grad, inputs, expert_ids, gate_weights, w_gate, w_up, w_down):
    devices = lax.axis_size("expert")
    spread = lax.axis_size("dp")
    experts = devices // HSPLIT
    tokens, features = out_grad.shape
    routed = expert_ids.shape[1]
    fold = fold_of(features)
    hidden = w_gate.shape[1]
    half = hidden // 2
    count = devices * CAP
    product = 2 * count * features * hidden
    dma = pltpu.SemaphoreType.DMA

    def to_expert(value, step):
        pairs = [(d, (d + step * HSPLIT) % devices) for d in range(devices)]
        return lax.ppermute(value, "expert", pairs)

    def to_peer(value, flip):
        return lax.ppermute(value, "expert", [(d, d ^ flip) for d in range(devices)])

    def to_dp(value, flip):
        return lax.ppermute(value, "dp", [(d, d ^ flip) for d in range(spread)])

    picked = run(
        functools.partial(pick_body, experts, fold),
        (shape((experts * fold * CAP, tokens)),) * fold
        + (shape((2 * CAP, features)),) * experts,
        [HBM] * 4,
        8 * experts * CAP * tokens * features,
        4 * tokens * features,
        *(in_hbm(array) for array in (expert_ids.T, gate_weights.T, out_grad, inputs)),
        scratch=(
            pltpu.VMEM((routed, tokens), jnp.int32),
            pltpu.VMEM((routed, tokens), F32),
            pltpu.VMEM((tokens, features), BF16),
            pltpu.VMEM((tokens, features), BF16),
            dma((2 + 2 * len(column_spans(features)),)),
        ),
    )
    picks, own = picked[:fold], picked[fold:]
    gate_here, up_here, down_across = run(
        functools.partial(load_body, 4),
        tuple(pltpu.VMEM(dims, BF16) for dims in (w_gate.shape, w_up.shape, w_down.shape[::-1])),
        [ANY] + [HBM] * 3,
        0,
        6 * features * hidden,
        picks[0],
        *(in_hbm(weight) for weight in (w_gate, w_up, w_down)),
        scratch=(pltpu.VMEM(w_down.shape, BF16), dma((12,))),
    )

    away = [to_expert(own[step], step) for step in range(1, experts)]
    near = [own[0]] + [to_peer(own[0], flip) for flip in range(1, HSPLIT)]
    away = away[0] if len(away) == 1 else jnp.concatenate(away, axis=0)
    far = [away] + [to_peer(away, flip) for flip in range(1, HSPLIT)]
    pieces = [array for pair in zip(near, far) for array in pair][::-1]

    rows_input, pre_send = run(
        pre_send_body,
        (shape((count, features)), shape((count, hidden))),
        [VMEM] * (2 + len(pieces)),
        product,
        4 * features * hidden,
        gate_here,
        up_here,
        *pieces,
    )
    rows_grad, hid_send = run(
        hidden_send_body,
        (shape((count, features)), shape((count, half))),
        [VMEM] * (1 + len(pieces)),
        product // 2,
        2 * features * hidden,
        down_across,
        *pieces,
    )
    pre_keep = run(
        pre_keep_body,
        shape((count, hidden)),
        [ANY] + [VMEM] * 3,
        0,
        0,
        hid_send,
        gate_here,
        up_here,
        rows_input,
    )
    hid_keep = run(
        hidden_keep_body,
        shape((count, half)),
        [VMEM] * 2,
        0,
        0,
        down_across,
        rows_grad,
    )

    def spread_sum(keep, send):
        near = (keep.astype(F32) + to_dp(send, 1).astype(F32)).astype(BF16)
        flip = 2
        far = jnp.zeros_like(near)
        while flip < spread:
            far = to_dp(near, flip)
            flip *= 2
            if flip < spread:
                near = (near.astype(F32) + far.astype(F32)).astype(BF16)
        return near, far

    pre_own, pre_far = spread_sum(pre_keep, pre_send)
    hid_own, hid_far = spread_sum(hid_keep, hid_send)
    rows_across, gate_across, up_across = run(
        transpose_body,
        (shape((features, count)),) + (shape((hidden, features)),) * 2,
        [ANY] + [VMEM] * 3,
        0,
        0,
        hid_own,
        rows_input,
        gate_here,
        up_here,
    )
    gate_acts, up_acts = run(
        activate_body,
        (shape((count, half)),) * 2,
        [ANY] + [VMEM] * 4,
        20 * count * half,
        10 * count * half,
        rows_across,
        pre_own,
        pre_far,
        hid_own,
        hid_far,
    )
    gate_other = to_dp(gate_acts, 1)
    up_other = to_dp(up_acts, 1)
    back_own = run(
        back_own_body,
        shape((count, features), F32),
        [VMEM] * 4,
        product,
        2 * features * hidden,
        gate_across,
        up_across,
        gate_acts,
        up_acts,
    )
    back_gate = run(
        back_gate_body,
        shape((count, features), F32),
        [VMEM] * 3,
        product // 2,
        features * hidden,
        gate_across,
        gate_other,
        back_own,
    )
    back = run(
        back_up_body,
        (shape((count // HSPLIT, features)),) * HSPLIT,
        [VMEM] * 3,
        product // 2,
        features * hidden,
        up_across,
        up_other,
        back_gate,
    )

    def weight_grad(acts, other, after):
        chunks = features // 256 if features % 256 == 0 else 2
        return run(
            functools.partial(weight_body, chunks),
            (shape((features, hidden)), shape((8, 128), F32)),
            [ANY] + [VMEM] * 3,
            0,
            0,
            after,
            rows_across,
            acts,
            other,
            out_spec=(HBM, VMEM),
            scratch=(pltpu.VMEM((features, hidden), BF16), dma((chunks,))),
        )

    grad_gate, token = weight_grad(gate_acts, gate_other, back[0])
    summed = run(
        functools.partial(gather_body, fold, experts),
        (shape((CAP * fold, features // fold)),) * experts,
        [ANY] + [VMEM] * HSPLIT,
        0,
        0,
        token,
        *(to_peer(back[flip], flip) for flip in range(HSPLIT - 1, 0, -1)),
        back[0],
    )
    grad_up, _ = weight_grad(up_acts, up_other, summed[0])
    returned = [summed[0]] + [to_expert(summed[step], experts - step) for step in range(1, experts)]
    in_grad = run(
        functools.partial(scatter_body, fold),
        shape((tokens, features)),
        [VMEM] * (fold + experts),
        4 * experts * CAP * tokens * features,
        2 * tokens * features,
        *picks,
        *returned,
        out_spec=HBM,
        scratch=(
            pltpu.VMEM((experts * fold * CAP, features // fold), F32),
            pltpu.VMEM((tokens, features), BF16),
            dma((fold * len(column_spans(features // fold)),)),
        ),
    )
    return (in_grad, grad_gate, grad_up)


def solution(mesh):
    placed = (
        P("expert", "dp"),
        P("expert", "dp"),
        P("expert", None),
        P("expert", None),
        P("dp", "expert"),
        P("dp", "expert"),
        P("expert", "dp"),
    )
    return jax.shard_map(
        per_device,
        mesh=mesh,
        in_specs=placed,
        out_specs=(P("expert", "dp"), P("dp", "expert"), P("dp", "expert")),
        check_vma=False,
    )
```

```python
import functools

import jax
import jax.numpy as jnp
from jax import lax
from jax.experimental import pallas as pl
from jax.experimental.pallas import tpu as pltpu
from jax.sharding import PartitionSpec as P

HSPLIT = 4
CAP = 12
F32 = jnp.float32
BF16 = jnp.bfloat16
VMEM = pl.BlockSpec(memory_space=pltpu.VMEM)
HBM = pl.BlockSpec(memory_space=pltpu.HBM)
ANY = pl.BlockSpec(memory_space=pl.ANY)


def shape(dims, dtype=BF16):
    return jax.ShapeDtypeStruct(dims, dtype)


def run(body, outs, specs, flops, nbytes, *args, out_spec=VMEM, scratch=()):
    return pl.pallas_call(
        body,
        out_shape=outs,
        in_specs=specs,
        out_specs=out_spec if isinstance(out_spec, tuple) else jax.tree.map(lambda _: out_spec, outs),
        scratch_shapes=scratch,
        compiler_params=pltpu.CompilerParams(vmem_limit_bytes=40 * 1024 * 1024),
        cost_estimate=pl.CostEstimate(flops=flops, bytes_accessed=nbytes, transcendentals=0),
    )(*args)


def in_hbm(value):
    return pltpu.with_memory_space_constraint(value, pltpu.HBM)


def dot(left, right, left_dim=1, right_dim=0):
    return lax.dot_general(
        left, right, (((left_dim,), (right_dim,)), ((), ())), preferred_element_type=F32
    )


def iota(dims, dim):
    return lax.broadcasted_iota(jnp.int32, dims, dim)


def over_cap(rows):
    return jnp.floor((rows.astype(F32) + 0.5) * (1.0 / CAP)).astype(jnp.int32)


def column_spans(width):
    whole = width // 128 * 128
    if whole != width or width < 512:
        return [slice(0, width)]
    middle = width // 256 * 128
    return [slice(0, middle), slice(middle, width)]


def core_columns(width, far):
    side = lax.rem(lax.axis_index("dp"), 2)
    side = 1 - side if far else side
    return pl.ds(pl.multiple_of(side * width, width), width)


def fold_of(width):
    return 2 if width % 256 == 0 else 1


def pick_body(experts, fold, ids_hbm, gates_hbm, grads_hbm, inputs_hbm, *refs):
    picks, pieces = refs[:fold], refs[fold : fold + experts]
    ids, gates, grads, inputs, sems = refs[fold + experts :]
    spans = column_spans(grads.shape[1])
    moves = [(ids_hbm, ids), (gates_hbm, gates)]
    for span in spans:
        moves.append((inputs_hbm.at[:, span], inputs.at[:, span]))
        moves.append((grads_hbm.at[:, span], grads.at[:, span]))
    loads = [
        pltpu.make_async_copy(source, target, sems.at[place])
        for place, (source, target) in enumerate(moves)
    ]
    for load in loads:
        load.start()
    tokens = ids.shape[1]
    padded = max(8, experts)
    group = lax.div(lax.axis_index("expert"), HSPLIT)
    earlier = (iota((tokens, tokens), 0) < iota((tokens, tokens), 1)).astype(F32).astype(BF16)
    loads[0].wait()
    loads[1].wait()
    expert_ids = ids[...]
    route_gates = gates[...]
    match_rows = jnp.zeros((padded, tokens), F32)
    matches = []
    token_gates = []
    for step in range(experts):
        hits = expert_ids == lax.rem(group + step, experts)
        match = jnp.sum(hits.astype(F32), axis=0, keepdims=True)
        matches.append(match)
        token_gates.append(jnp.sum(jnp.where(hits, route_gates, 0.0), axis=0, keepdims=True))
        match_rows = jnp.where(iota((padded, tokens), 0) == step, match, match_rows)
    counts = dot(match_rows.astype(BF16), earlier)
    slots = [
        jnp.where(matches[step] > 0.0, counts[step : step + 1, :], -1.0e6)
        for step in range(experts)
    ]

    def chosen(rows, offset):
        places = (iota((rows, tokens), 0) - offset).astype(F32)
        return [(places == slots[step]).astype(F32) for step in range(experts)]

    input_picks = chosen(2 * CAP, 0)
    grad_picks = chosen(2 * CAP, CAP)
    slot_gates = [
        jnp.sum(hit * gate, axis=1, keepdims=True) for hit, gate in zip(grad_picks, token_gates)
    ]
    gate_column = jnp.concatenate(slot_gates, axis=0)
    input_picks = jnp.concatenate(input_picks, axis=0)
    grad_picks = jnp.concatenate(grad_picks, axis=0)
    if fold == 2:
        picks[0][...] = input_picks.astype(BF16)
        picks[1][...] = grad_picks.astype(BF16)
    else:
        picks[0][...] = jnp.concatenate(chosen(CAP, 0), axis=0).astype(BF16)
    input_picks = input_picks.astype(BF16)
    grad_picks = grad_picks.astype(BF16)
    for place, span in enumerate(spans):
        loads[2 + 2 * place].wait()
        total = dot(input_picks, inputs[:, span])
        loads[3 + 2 * place].wait()
        total = total + dot(grad_picks, grads[:, span]) * gate_column
        for step in range(experts):
            rows = slice(step * 2 * CAP, (step + 1) * 2 * CAP)
            pieces[step][:, span] = total[rows].astype(BF16)


def load_body(parts, after, *refs):
    hbm, (w_gate, w_up, down_across, w_down, sems) = refs[:3], refs[3:]
    loads = []
    for source, target in zip((hbm[2], hbm[0], hbm[1]), (w_down, w_gate, w_up)):
        depth = source.shape[0] // parts
        for part in range(parts):
            rows = slice(part * depth, (part + 1) * depth)
            loads.append(
                pltpu.make_async_copy(source.at[rows], target.at[rows], sems.at[len(loads)])
            )
    for load in loads:
        load.start()
    for load in loads[:parts]:
        load.wait()
    down_across[...] = w_down[...].T
    for load in loads[parts:]:
        load.wait()


def take_rows(offset, pieces):
    rows = []
    far, near = pieces[:HSPLIT][::-1], pieces[-1:] + pieces[HSPLIT:-1]
    for ref in [ref for pair in zip(near, far) for ref in pair]:
        piece = ref[...].astype(F32)
        for place in range(offset, piece.shape[0], 2 * CAP):
            rows.append(piece[place : place + CAP])
    return jnp.concatenate(rows, axis=0).astype(BF16)


def forward_body(w_gate, w_up, *refs):
    pieces, (rows_out, keep, send) = refs[:-3], refs[-3:]
    half = w_gate.shape[1] // 2
    rows = take_rows(0, pieces)
    rows_out[...] = rows
    for target, far in ((send, True), (keep, False)):
        columns = core_columns(half, far)
        target[:, :half] = dot(rows, w_gate[:, columns]).astype(BF16)
        target[:, half:] = dot(rows, w_up[:, columns]).astype(BF16)


def hidden_body(down_across, *refs):
    pieces, (keep, send) = refs[:-2], refs[-2:]
    half = down_across.shape[1] // 2
    rows = take_rows(CAP, pieces)
    for target, far in ((send, True), (keep, False)):
        target[...] = dot(rows, down_across[:, core_columns(half, far)]).astype(BF16)


def transpose_body(after, rows_ref, w_gate, w_up, rows_across, gate_across, up_across):
    rows = rows_ref[...]
    count = rows.shape[0]
    same = (iota((count, count), 0) == iota((count, count), 1)).astype(F32).astype(BF16)
    rows_across[...] = dot(rows, same, 0, 0).astype(BF16)
    gate_across[...] = w_gate[...].T
    up_across[...] = w_up[...].T


def activate_body(after, pre_own, pre_far, hid_own, hid_far, acts):
    half = hid_own.shape[1]
    pre = pre_own[...].astype(F32) + pre_far[...].astype(F32)
    hidden_grad = hid_own[...].astype(F32) + hid_far[...].astype(F32)
    gate_pre = pre[:, :half]
    up_pre = pre[:, half:]
    sigma = jax.nn.sigmoid(gate_pre)
    acts[:, :half] = (hidden_grad * up_pre * sigma * (1.0 + gate_pre * (1.0 - sigma))).astype(BF16)
    acts[:, half:] = (hidden_grad * gate_pre * sigma).astype(BF16)


def fold_rows(rows, fold):
    width = rows.shape[1] // fold
    return [
        jnp.concatenate(
            [rows[place : place + CAP, part * width : (part + 1) * width] for part in range(fold)],
            axis=0,
        )
        for place in range(0, rows.shape[0], CAP)
    ]


def back_part(gate_across, up_across, acts, sibling):
    half = gate_across.shape[0] // 2
    units = core_columns(half, sibling)
    part = dot(acts[:, :half], gate_across[units, :])
    return part + dot(acts[:, half:], up_across[units, :])


def back_own_body(gate_across, up_across, acts, total):
    total[...] = back_part(gate_across, up_across, acts, False)


def back_far_body(gate_across, up_across, acts, own, *outs):
    count = outs[0].shape[0]
    total = own[...] + back_part(gate_across, up_across, acts, True)
    for place, out in enumerate(outs):
        out[...] = total[place * count : (place + 1) * count].astype(BF16)


def weight_body(which, chunks, after, rows_ref, acts_own, acts_far, out, token, tile, sems):
    token[...] = jnp.zeros_like(token)
    half = out.shape[1] // 2
    depth = out.shape[0] // chunks
    columns = slice(which * half, (which + 1) * half)
    stores = []
    for chunk in range(chunks):
        span = slice(chunk * depth, (chunk + 1) * depth)
        rows = rows_ref[span, :]
        for acts, far in ((acts_own, False), (acts_far, True)):
            tile[span, core_columns(half, far)] = dot(rows, acts[:, columns]).astype(BF16)
        stores.append(pltpu.make_async_copy(tile.at[span], out.at[span], sems.at[chunk]))
        stores[-1].start()
    for store in stores:
        store.wait()


def gather_body(fold, experts, after, *refs):
    parts, outs = refs[:HSPLIT], refs[HSPLIT:]
    total = parts[0][...].astype(F32) + parts[1][...].astype(F32)
    total = total + (parts[2][...].astype(F32) + parts[3][...].astype(F32))
    for out, rows in zip(outs, fold_rows(total, fold)):
        out[...] = rows.astype(BF16)


def scatter_body(fold, *refs):
    picks, pieces = refs[:fold], refs[fold:-4]
    out, stack, tile, sems = refs[-4:]
    width = out.shape[1] // fold
    piece = CAP * fold
    for place, ref in enumerate(pieces):
        stack[place * piece : (place + 1) * piece, :] = ref[...].astype(F32)
    returned = stack[...].astype(BF16)
    stores = []
    for part in range(fold):
        for span in column_spans(width):
            target = slice(part * width + span.start, part * width + span.stop)
            tile[:, target] = dot(picks[part][...], returned[:, span], 0, 0).astype(BF16)
            store = pltpu.make_async_copy(
                tile.at[:, target], out.at[:, target], sems.at[len(stores)]
            )
            store.start()
            stores.append(store)
    for store in stores:
        store.wait()


def per_device(out_grad, inputs, expert_ids, gate_weights, w_gate, w_up, w_down):
    devices = lax.axis_size("expert")
    spread = lax.axis_size("dp")
    experts = devices // HSPLIT
    tokens, features = out_grad.shape
    routed = expert_ids.shape[1]
    fold = fold_of(features)
    hidden = w_gate.shape[1]
    half = hidden // 2
    count = devices * CAP
    product = 2 * count * features * hidden
    dma = pltpu.SemaphoreType.DMA

    def to_expert(value, step):
        pairs = [(d, (d + step * HSPLIT) % devices) for d in range(devices)]
        return lax.ppermute(value, "expert", pairs)

    def to_peer(value, flip):
        return lax.ppermute(value, "expert", [(d, d ^ flip) for d in range(devices)])

    def to_dp(value, flip):
        return lax.ppermute(value, "dp", [(d, d ^ flip) for d in range(spread)])

    picked = run(
        functools.partial(pick_body, experts, fold),
        (shape((experts * fold * CAP, tokens)),) * fold
        + (shape((2 * CAP, features)),) * experts,
        [HBM] * 4,
        8 * experts * CAP * tokens * features,
        4 * tokens * features,
        *(in_hbm(array) for array in (expert_ids.T, gate_weights.T, out_grad, inputs)),
        scratch=(
            pltpu.VMEM((routed, tokens), jnp.int32),
            pltpu.VMEM((routed, tokens), F32),
            pltpu.VMEM((tokens, features), BF16),
            pltpu.VMEM((tokens, features), BF16),
            dma((2 + 2 * len(column_spans(features)),)),
        ),
    )
    picks, own = picked[:fold], picked[fold:]
    gate_here, up_here, down_across = run(
        functools.partial(load_body, 4),
        tuple(pltpu.VMEM(dims, BF16) for dims in (w_gate.shape, w_up.shape, w_down.shape[::-1])),
        [ANY] + [HBM] * 3,
        0,
        6 * features * hidden,
        picks[0],
        *(in_hbm(weight) for weight in (w_gate, w_up, w_down)),
        scratch=(pltpu.VMEM(w_down.shape, BF16), dma((12,))),
    )

    away = [to_expert(own[step], step) for step in range(1, experts)]
    near = [own[0]] + [to_peer(own[0], flip) for flip in range(1, HSPLIT)]
    away = away[0] if len(away) == 1 else jnp.concatenate(away, axis=0)
    far = [away] + [to_peer(away, flip) for flip in range(1, HSPLIT)]
    pieces = far[::-1] + near[1:] + near[:1]

    rows_input, pre_keep, pre_send = run(
        forward_body,
        (shape((count, features)), shape((count, hidden)), shape((count, hidden))),
        [VMEM] * (2 + len(pieces)),
        2 * product,
        4 * features * hidden,
        gate_here,
        up_here,
        *pieces,
    )

    def spread_sum(keep, send):
        near = (keep.astype(F32) + to_dp(send, 1).astype(F32)).astype(BF16)
        flip = 2
        far = jnp.zeros_like(near)
        while flip < spread:
            far = to_dp(near, flip)
            flip *= 2
            if flip < spread:
                near = (near.astype(F32) + far.astype(F32)).astype(BF16)
        return near, far

    pre_own, pre_far = spread_sum(pre_keep, pre_send)
    hid_keep, hid_send = run(
        hidden_body,
        (shape((count, half)), shape((count, half))),
        [VMEM] * (1 + len(pieces)),
        product,
        2 * features * hidden,
        down_across,
        *pieces,
    )
    hid_own, hid_far = spread_sum(hid_keep, hid_send)
    rows_across, gate_across, up_across = run(
        transpose_body,
        (shape((features, count)),) + (shape((hidden, features)),) * 2,
        [ANY] + [VMEM] * 3,
        0,
        0,
        hid_own,
        rows_input,
        gate_here,
        up_here,
    )
    acts = run(
        activate_body,
        shape((count, hidden)),
        [ANY] + [VMEM] * 4,
        20 * count * half,
        10 * count * half,
        rows_across,
        pre_own,
        pre_far,
        hid_own,
        hid_far,
    )
    acts_far = to_dp(acts, 1)
    back_own = run(
        back_own_body,
        shape((count, features), F32),
        [VMEM] * 3,
        product,
        2 * features * hidden,
        gate_across,
        up_across,
        acts,
    )
    back = run(
        back_far_body,
        (shape((count // HSPLIT, features)),) * HSPLIT,
        [VMEM] * 4,
        product,
        2 * features * hidden,
        gate_across,
        up_across,
        acts_far,
        back_own,
    )

    def weight_grad(which, after):
        chunks = features // 256 if features % 256 == 0 else 2
        return run(
            functools.partial(weight_body, which, chunks),
            (shape((features, hidden)), shape((8, 128), F32)),
            [ANY] + [VMEM] * 3,
            0,
            0,
            after,
            rows_across,
            acts,
            acts_far,
            out_spec=(HBM, VMEM),
            scratch=(pltpu.VMEM((features, hidden), BF16), dma((chunks,))),
        )

    grad_gate, token = weight_grad(0, back[0])
    grad_up, token = weight_grad(1, token)
    summed = run(
        functools.partial(gather_body, fold, experts),
        (shape((CAP * fold, features // fold)),) * experts,
        [ANY] + [VMEM] * HSPLIT,
        0,
        0,
        token,
        *(to_peer(back[flip], flip) for flip in range(HSPLIT - 1, 0, -1)),
        back[0],
    )
    returned = [summed[0]] + [to_expert(summed[step], experts - step) for step in range(1, experts)]
    in_grad = run(
        functools.partial(scatter_body, fold),
        shape((tokens, features)),
        [VMEM] * (fold + experts),
        4 * experts * CAP * tokens * features,
        2 * tokens * features,
        *picks,
        *returned,
        out_spec=HBM,
        scratch=(
            pltpu.VMEM((experts * fold * CAP, features // fold), F32),
            pltpu.VMEM((tokens, features), BF16),
            dma((fold * len(column_spans(features // fold)),)),
        ),
    )
    return (in_grad, grad_gate, grad_up)


def solution(mesh):
    placed = (
        P("expert", "dp"),
        P("expert", "dp"),
        P("expert", None),
        P("expert", None),
        P("dp", "expert"),
        P("dp", "expert"),
        P("expert", "dp"),
    )
    return jax.shard_map(
        per_device,
        mesh=mesh,
        in_specs=placed,
        out_specs=(P("expert", "dp"), P("dp", "expert"), P("dp", "expert")),
        check_vma=False,
    )
```

```python
import functools

import jax
import jax.numpy as jnp
from jax import lax
from jax.experimental import pallas as pl
from jax.experimental.pallas import tpu as pltpu
from jax.sharding import PartitionSpec as P

HSPLIT = 4
CAP = 12
F32 = jnp.float32
BF16 = jnp.bfloat16
VMEM = pl.BlockSpec(memory_space=pltpu.VMEM)
HBM = pl.BlockSpec(memory_space=pltpu.HBM)
ANY = pl.BlockSpec(memory_space=pl.ANY)


def shape(dims, dtype=BF16):
    return jax.ShapeDtypeStruct(dims, dtype)


def run(body, outs, specs, flops, nbytes, *args, out_spec=VMEM, scratch=()):
    return pl.pallas_call(
        body,
        out_shape=outs,
        in_specs=specs,
        out_specs=out_spec if isinstance(out_spec, tuple) else jax.tree.map(lambda _: out_spec, outs),
        scratch_shapes=scratch,
        compiler_params=pltpu.CompilerParams(vmem_limit_bytes=40 * 1024 * 1024),
        cost_estimate=pl.CostEstimate(flops=flops, bytes_accessed=nbytes, transcendentals=0),
    )(*args)


def in_hbm(value):
    return pltpu.with_memory_space_constraint(value, pltpu.HBM)


def dot(left, right, left_dim=1, right_dim=0):
    return lax.dot_general(
        left, right, (((left_dim,), (right_dim,)), ((), ())), preferred_element_type=F32
    )


def iota(dims, dim):
    return lax.broadcasted_iota(jnp.int32, dims, dim)


def over_cap(rows):
    return jnp.floor((rows.astype(F32) + 0.5) * (1.0 / CAP)).astype(jnp.int32)


def column_spans(width):
    whole = width // 128 * 128
    if whole != width or width < 512:
        return [slice(0, width)]
    middle = width // 256 * 128
    return [slice(0, middle), slice(middle, width)]


def core_columns(width, far):
    side = lax.rem(lax.axis_index("dp"), 2)
    side = 1 - side if far else side
    return pl.ds(pl.multiple_of(side * width, width), width)


def fold_of(width):
    return 2 if width % 256 == 0 else 1


def pick_body(experts, fold, ids_hbm, gates_hbm, grads_hbm, inputs_hbm, *refs):
    picks, pieces = refs[:fold], refs[fold : fold + experts]
    ids, gates, grads, inputs, sems = refs[fold + experts :]
    spans = column_spans(grads.shape[1])
    moves = [(ids_hbm, ids), (gates_hbm, gates)]
    for span in spans:
        moves.append((inputs_hbm.at[:, span], inputs.at[:, span]))
        moves.append((grads_hbm.at[:, span], grads.at[:, span]))
    loads = [
        pltpu.make_async_copy(source, target, sems.at[place])
        for place, (source, target) in enumerate(moves)
    ]
    for load in loads:
        load.start()
    tokens = ids.shape[1]
    padded = max(8, experts)
    group = lax.div(lax.axis_index("expert"), HSPLIT)
    earlier = (iota((tokens, tokens), 0) < iota((tokens, tokens), 1)).astype(F32).astype(BF16)
    loads[0].wait()
    loads[1].wait()
    expert_ids = ids[...]
    route_gates = gates[...]
    match_rows = jnp.zeros((padded, tokens), F32)
    matches = []
    token_gates = []
    for step in range(experts):
        hits = expert_ids == lax.rem(group + step, experts)
        match = jnp.sum(hits.astype(F32), axis=0, keepdims=True)
        matches.append(match)
        token_gates.append(jnp.sum(jnp.where(hits, route_gates, 0.0), axis=0, keepdims=True))
        match_rows = jnp.where(iota((padded, tokens), 0) == step, match, match_rows)
    counts = dot(match_rows.astype(BF16), earlier)
    slots = [
        jnp.where(matches[step] > 0.0, counts[step : step + 1, :], -1.0e6)
        for step in range(experts)
    ]

    def chosen(rows, offset):
        places = (iota((rows, tokens), 0) - offset).astype(F32)
        return [(places == slots[step]).astype(F32) for step in range(experts)]

    input_picks = chosen(2 * CAP, 0)
    grad_picks = chosen(2 * CAP, CAP)
    slot_gates = [
        jnp.sum(hit * gate, axis=1, keepdims=True) for hit, gate in zip(grad_picks, token_gates)
    ]
    gate_column = jnp.concatenate(slot_gates, axis=0)
    input_picks = jnp.concatenate(input_picks, axis=0)
    grad_picks = jnp.concatenate(grad_picks, axis=0)
    if fold == 2:
        picks[0][...] = input_picks.astype(BF16)
        picks[1][...] = grad_picks.astype(BF16)
    else:
        picks[0][...] = jnp.concatenate(chosen(CAP, 0), axis=0).astype(BF16)
    input_picks = input_picks.astype(BF16)
    grad_picks = grad_picks.astype(BF16)
    for place, span in enumerate(spans):
        loads[2 + 2 * place].wait()
        total = dot(input_picks, inputs[:, span])
        loads[3 + 2 * place].wait()
        total = total + dot(grad_picks, grads[:, span]) * gate_column
        for step in range(experts):
            rows = slice(step * 2 * CAP, (step + 1) * 2 * CAP)
            pieces[step][:, span] = total[rows].astype(BF16)


def load_body(parts, after, *refs):
    hbm, (w_gate, w_up, down_across, w_down, sems) = refs[:3], refs[3:]
    loads = []
    for source, target in zip((hbm[2], hbm[0], hbm[1]), (w_down, w_gate, w_up)):
        depth = source.shape[0] // parts
        for part in range(parts):
            rows = slice(part * depth, (part + 1) * depth)
            loads.append(
                pltpu.make_async_copy(source.at[rows], target.at[rows], sems.at[len(loads)])
            )
    for load in loads:
        load.start()
    for load in loads[:parts]:
        load.wait()
    down_across[...] = w_down[...].T
    for load in loads[parts:]:
        load.wait()


def take_rows(offset, pieces):
    rows = []
    far, near = pieces[:HSPLIT][::-1], pieces[-1:] + pieces[HSPLIT:-1]
    for ref in [ref for pair in zip(near, far) for ref in pair]:
        piece = ref[...].astype(F32)
        for place in range(offset, piece.shape[0], 2 * CAP):
            rows.append(piece[place : place + CAP])
    return jnp.concatenate(rows, axis=0).astype(BF16)


def forward_body(w_gate, w_up, *refs):
    pieces, (rows_out, keep, send) = refs[:-3], refs[-3:]
    half = w_gate.shape[1] // 2
    rows = take_rows(0, pieces)
    rows_out[...] = rows
    for target, far in ((send, True), (keep, False)):
        columns = core_columns(half, far)
        target[:, :half] = dot(rows, w_gate[:, columns]).astype(BF16)
        target[:, half:] = dot(rows, w_up[:, columns]).astype(BF16)


def hidden_body(down_across, *refs):
    pieces, (keep, send) = refs[:-2], refs[-2:]
    half = down_across.shape[1] // 2
    rows = take_rows(CAP, pieces)
    for target, far in ((send, True), (keep, False)):
        target[...] = dot(rows, down_across[:, core_columns(half, far)]).astype(BF16)


def transpose_body(after, rows_ref, w_gate, w_up, *refs):
    count = (len(refs) - 3) // 2
    picks, (rows_across, gate_across, up_across) = refs[:count], refs[count : count + 3]
    for pick, across in zip(picks, refs[count + 3 :]):
        across[...] = pick[...].astype(F32).T.astype(BF16)
    rows = rows_ref[...]
    count = rows.shape[0]
    same = (iota((count, count), 0) == iota((count, count), 1)).astype(F32).astype(BF16)
    rows_across[...] = dot(rows, same, 0, 0).astype(BF16)
    gate_across[...] = w_gate[...].T
    up_across[...] = w_up[...].T


def activate_body(after, pre_own, pre_far, hid_own, hid_far, acts):
    half = hid_own.shape[1]
    pre = pre_own[...].astype(F32) + pre_far[...].astype(F32)
    hidden_grad = hid_own[...].astype(F32) + hid_far[...].astype(F32)
    gate_pre = pre[:, :half]
    up_pre = pre[:, half:]
    sigma = jax.nn.sigmoid(gate_pre)
    acts[:, :half] = (hidden_grad * up_pre * sigma * (1.0 + gate_pre * (1.0 - sigma))).astype(BF16)
    acts[:, half:] = (hidden_grad * gate_pre * sigma).astype(BF16)


def fold_rows(rows, fold):
    width = rows.shape[1] // fold
    return [
        jnp.concatenate(
            [rows[place : place + CAP, part * width : (part + 1) * width] for part in range(fold)],
            axis=0,
        )
        for place in range(0, rows.shape[0], CAP)
    ]


def back_part(gate_across, up_across, acts, sibling):
    half = gate_across.shape[0] // 2
    units = core_columns(half, sibling)
    part = dot(acts[:, :half], gate_across[units, :])
    return part + dot(acts[:, half:], up_across[units, :])


def back_own_body(gate_across, up_across, acts, total):
    total[...] = back_part(gate_across, up_across, acts, False)


def back_far_body(gate_across, up_across, acts, own, *outs):
    count = outs[0].shape[0]
    total = own[...] + back_part(gate_across, up_across, acts, True)
    for place, out in enumerate(outs):
        out[...] = total[place * count : (place + 1) * count].astype(BF16)


def weight_body(which, chunks, after, rows_ref, acts_own, acts_far, out, token, tile, sems):
    token[...] = jnp.zeros_like(token)
    half = out.shape[1] // 2
    depth = out.shape[0] // chunks
    columns = slice(which * half, (which + 1) * half)
    stores = []
    for chunk in range(chunks):
        span = slice(chunk * depth, (chunk + 1) * depth)
        rows = rows_ref[span, :]
        for acts, far in ((acts_own, False), (acts_far, True)):
            tile[span, core_columns(half, far)] = dot(rows, acts[:, columns]).astype(BF16)
        stores.append(pltpu.make_async_copy(tile.at[span], out.at[span], sems.at[chunk]))
        stores[-1].start()
    for store in stores:
        store.wait()


def gather_body(fold, experts, after, *refs):
    parts, outs = refs[:HSPLIT], refs[HSPLIT:]
    total = parts[0][...].astype(F32) + parts[1][...].astype(F32)
    total = total + (parts[2][...].astype(F32) + parts[3][...].astype(F32))
    for out, rows in zip(outs, fold_rows(total, fold)):
        out[...] = rows.astype(BF16)


def scatter_body(fold, *refs):
    picks, pieces = refs[:fold], refs[fold:-4]
    out, stack, tile, sems = refs[-4:]
    width = out.shape[1] // fold
    piece = CAP * fold
    for place, ref in enumerate(pieces):
        stack[place * piece : (place + 1) * piece, :] = ref[...].astype(F32)
    returned = stack[...].astype(BF16)
    stores = []
    for part in range(fold):
        for span in column_spans(width):
            target = slice(part * width + span.start, part * width + span.stop)
            tile[:, target] = dot(picks[part][...], returned[:, span]).astype(BF16)
            store = pltpu.make_async_copy(
                tile.at[:, target], out.at[:, target], sems.at[len(stores)]
            )
            store.start()
            stores.append(store)
    for store in stores:
        store.wait()


def per_device(out_grad, inputs, expert_ids, gate_weights, w_gate, w_up, w_down):
    devices = lax.axis_size("expert")
    spread = lax.axis_size("dp")
    experts = devices // HSPLIT
    tokens, features = out_grad.shape
    routed = expert_ids.shape[1]
    fold = fold_of(features)
    hidden = w_gate.shape[1]
    half = hidden // 2
    count = devices * CAP
    product = 2 * count * features * hidden
    dma = pltpu.SemaphoreType.DMA

    def to_expert(value, step):
        pairs = [(d, (d + step * HSPLIT) % devices) for d in range(devices)]
        return lax.ppermute(value, "expert", pairs)

    def to_peer(value, flip):
        return lax.ppermute(value, "expert", [(d, d ^ flip) for d in range(devices)])

    def to_dp(value, flip):
        return lax.ppermute(value, "dp", [(d, d ^ flip) for d in range(spread)])

    picked = run(
        functools.partial(pick_body, experts, fold),
        (shape((experts * fold * CAP, tokens)),) * fold
        + (shape((2 * CAP, features)),) * experts,
        [HBM] * 4,
        8 * experts * CAP * tokens * features,
        4 * tokens * features,
        *(in_hbm(array) for array in (expert_ids.T, gate_weights.T, out_grad, inputs)),
        scratch=(
            pltpu.VMEM((routed, tokens), jnp.int32),
            pltpu.VMEM((routed, tokens), F32),
            pltpu.VMEM((tokens, features), BF16),
            pltpu.VMEM((tokens, features), BF16),
            dma((2 + 2 * len(column_spans(features)),)),
        ),
    )
    picks, own = picked[:fold], picked[fold:]
    gate_here, up_here, down_across = run(
        functools.partial(load_body, 4),
        tuple(pltpu.VMEM(dims, BF16) for dims in (w_gate.shape, w_up.shape, w_down.shape[::-1])),
        [ANY] + [HBM] * 3,
        0,
        6 * features * hidden,
        picks[0],
        *(in_hbm(weight) for weight in (w_gate, w_up, w_down)),
        scratch=(pltpu.VMEM(w_down.shape, BF16), dma((12,))),
    )

    away = [to_expert(own[step], step) for step in range(1, experts)]
    near = [own[0]] + [to_peer(own[0], flip) for flip in range(1, HSPLIT)]
    away = away[0] if len(away) == 1 else jnp.concatenate(away, axis=0)
    far = [away] + [to_peer(away, flip) for flip in range(1, HSPLIT)]
    pieces = far[::-1] + near[1:] + near[:1]

    rows_input, pre_keep, pre_send = run(
        forward_body,
        (shape((count, features)), shape((count, hidden)), shape((count, hidden))),
        [VMEM] * (2 + len(pieces)),
        2 * product,
        4 * features * hidden,
        gate_here,
        up_here,
        *pieces,
    )

    def spread_sum(keep, send):
        near = (keep.astype(F32) + to_dp(send, 1).astype(F32)).astype(BF16)
        flip = 2
        far = jnp.zeros_like(near)
        while flip < spread:
            far = to_dp(near, flip)
            flip *= 2
            if flip < spread:
                near = (near.astype(F32) + far.astype(F32)).astype(BF16)
        return near, far

    pre_own, pre_far = spread_sum(pre_keep, pre_send)
    hid_keep, hid_send = run(
        hidden_body,
        (shape((count, half)), shape((count, half))),
        [VMEM] * (1 + len(pieces)),
        product,
        2 * features * hidden,
        down_across,
        *pieces,
    )
    hid_own, hid_far = spread_sum(hid_keep, hid_send)
    rows_across, gate_across, up_across, *picks_across = run(
        transpose_body,
        (shape((features, count)),)
        + (shape((hidden, features)),) * 2
        + tuple(shape(pick.shape[::-1]) for pick in picks),
        [ANY] + [VMEM] * (3 + fold),
        0,
        0,
        hid_own,
        rows_input,
        gate_here,
        up_here,
        *picks,
    )
    acts = run(
        activate_body,
        shape((count, hidden)),
        [ANY] + [VMEM] * 4,
        20 * count * half,
        10 * count * half,
        rows_across,
        pre_own,
        pre_far,
        hid_own,
        hid_far,
    )
    acts_far = to_dp(acts, 1)
    back_own = run(
        back_own_body,
        shape((count, features), F32),
        [VMEM] * 3,
        product,
        2 * features * hidden,
        gate_across,
        up_across,
        acts,
    )
    back = run(
        back_far_body,
        (shape((count // HSPLIT, features)),) * HSPLIT,
        [VMEM] * 4,
        product,
        2 * features * hidden,
        gate_across,
        up_across,
        acts_far,
        back_own,
    )

    def weight_grad(which, after):
        chunks = features // 256 if features % 256 == 0 else 2
        return run(
            functools.partial(weight_body, which, chunks),
            (shape((features, hidden)), shape((8, 128), F32)),
            [ANY] + [VMEM] * 3,
            0,
            0,
            after,
            rows_across,
            acts,
            acts_far,
            out_spec=(HBM, VMEM),
            scratch=(pltpu.VMEM((features, hidden), BF16), dma((chunks,))),
        )

    grad_gate, token = weight_grad(0, back[0])
    grad_up, token = weight_grad(1, token)
    summed = run(
        functools.partial(gather_body, fold, experts),
        (shape((CAP * fold, features // fold)),) * experts,
        [ANY] + [VMEM] * HSPLIT,
        0,
        0,
        token,
        *(to_peer(back[flip], flip) for flip in range(HSPLIT - 1, 0, -1)),
        back[0],
    )
    returned = [summed[0]] + [to_expert(summed[step], experts - step) for step in range(1, experts)]
    in_grad = run(
        functools.partial(scatter_body, fold),
        shape((tokens, features)),
        [VMEM] * (fold + experts),
        4 * experts * CAP * tokens * features,
        2 * tokens * features,
        *picks_across,
        *returned,
        out_spec=HBM,
        scratch=(
            pltpu.VMEM((experts * fold * CAP, features // fold), F32),
            pltpu.VMEM((tokens, features), BF16),
            dma((fold * len(column_spans(features // fold)),)),
        ),
    )
    return (in_grad, grad_gate, grad_up)


def solution(mesh):
    placed = (
        P("expert", "dp"),
        P("expert", "dp"),
        P("expert", None),
        P("expert", None),
        P("dp", "expert"),
        P("dp", "expert"),
        P("expert", "dp"),
    )
    return jax.shard_map(
        per_device,
        mesh=mesh,
        in_specs=placed,
        out_specs=(P("expert", "dp"), P("dp", "expert"), P("dp", "expert")),
        check_vma=False,
    )
```
